32 devices in a mesh: shot: 2 (over y), gx: 4 (over z), gy: 4 (over x, core).
Axes of the slice: x: 2, y: 2, z: 4, core: 2. Of those that a mesh axis runs over, the one named last changes fastest.
Arguments:
- vel_coef: float32 [128, 128, 128], P('gx', 'gy'), may hold values from 0.03 to 0.2
- src_prev: float32 [2, 128, 128, 128], P('shot', 'gx', 'gy'), may hold values from -6 to 6
- src_cur: float32 [2, 128, 128, 128], P('shot', 'gx', 'gy'), may hold values from -6 to 6
- rcv_prev: float32 [2, 128, 128, 128], P('shot', 'gx', 'gy'), may hold values from -6 to 6
- rcv_cur: float32 [2, 128, 128, 128], P('shot', 'gx', 'gy'), may hold values from -6 to 6
- src_pos: int32 [2], P('shot'), may hold values from 0 to 2097151
- src_amp: float32 [2, 3], P('shot'), may hold values from -24 to 24
- rcv_pos: int32 [2, 512], P('shot'), may hold values from 0 to 2097151
- rcv_data: float32 [2, 3, 512], P('shot'), may hold values from -6 to 6
- aperture: int32 [2, 8], P('shot'), may hold values from 0 to 15, as said below
- owner: int32 [16, 16], replicated, may hold values from 0 to 15, as said below
Outputs:
- src_next: float32 [2, 128, 128, 128], P('shot', 'gx', 'gy')
- rcv_next: float32 [2, 128, 128, 128], P('shot', 'gx', 'gy')
- gathers: float32 [16, 16, 16, 2, 32, 128], P(('gx', 'gy'), 'shot')
The draws below stay inside these ranges and needn't reach their ends.
Inputs may be any that keep to these rules, and one draw needn't show every extreme that they name: `aperture`: each row lists 8 different tiles. `owner`: each row and each column holds every tile number once.
All inputs are finite; a program needn't handle non-finite values.
Results may differ from the reference program's by a relative error of at most 0.0003.
Values sent between devices are 32-bit elements; how exact they have to be, the bound alone decides.
No kernel may reach another device: no remote copies, remote signals or barrier semaphores. Data moves between devices by JAX's collectives and lax.ppermute only.
A program may use at most 64 MiB of HBM per device.

```python
import math
import jax
import jax.numpy as jnp
from jax import lax

CX = 32
CY = 32
OFFS = 16
STEPS = 3
RCV = 512
HALF = 8
SHOTS = 2
NT = 16
NAP = 8
SX = 2
NX = 128
NY = 128
NZ = 128
N_GX = 4
N_GY = 4


def draw_aperture(key, part):
    shot_keys = jax.random.split(jax.random.fold_in(key, 11), SHOTS)

    def choose_tiles(one_key):
        return jax.random.permutation(one_key, NT)[:NAP]
    return jax.vmap(choose_tiles)(shot_keys).astype(jnp.int32)


def draw_owner(key, part):
    relabel = jax.random.permutation(jax.random.fold_in(key, 21), NT)
    second = jax.random.permutation(jax.random.fold_in(key, 22), NT)
    row_index = jnp.arange(NT)[:, None]
    return relabel[(second[None, :] + row_index) % NT].astype(jnp.int32)


def plant(result, key, smallest, top_value):
    longest = result.shape.index(max(result.shape))
    spots = []
    for shift in (0, 1):
        where = [jax.random.randint(jax.random.fold_in(key, axis), (), 0, length) for axis, length in enumerate(result.shape)]
        where[longest] = (where[longest] + shift) % result.shape[longest]
        spots.append(tuple(where))
    return result.at[spots[0]].set(smallest).at[spots[1]].set(top_value)


def shard_levels(key, extent, pieces, smallest, largest):
    def one(position, blocks):
        steps = jax.random.uniform(jax.random.fold_in(jax.random.fold_in(key, 6), position), (blocks,), jnp.float32, smallest / len(pieces), largest / len(pieces))
        return jnp.repeat(jnp.exp(steps), extent[position] // blocks).reshape((-1,) + (1,) * (len(extent) - position - 1))

    level = one(*pieces[0])
    for cut in pieces[1:]:
        level = level * one(*cut)
    return level


def centred(own_key, shape, width, reach, shards=(), kind=jnp.bfloat16):
    factor_of = shard_levels(own_key, shape, shards, -0.22, 0.18) if shards else 1.0
    array = jax.random.normal(own_key, shape, jnp.float32) * width * factor_of
    return jnp.minimum(jnp.maximum(array, -reach), reach).astype(kind)


def setup_inputs(seed: int = 0) -> dict:
    keys = jax.random.split(jax.random.key(seed), 12)
    return {
        "vel_coef": jnp.clip(jnp.exp(math.log(0.2) - 1.89712 * jax.random.uniform(keys[0], (NX, NY, NZ), jnp.float32) ** shard_levels(keys[0], (NX, NY, NZ), ((0, 4), (1, 4)), -0.2, 0.2)), 0.03, 0.2),
        "src_prev": centred(keys[1], (SHOTS, NX, NY, NZ), 1.0, 6.0, ((0, 2), (1, 4), (2, 4)), jnp.float32),
        "src_cur": centred(keys[2], (SHOTS, NX, NY, NZ), 1.0, 6.0, ((0, 2), (1, 4), (2, 4)), jnp.float32),
        "rcv_prev": centred(keys[3], (SHOTS, NX, NY, NZ), 1.0, 6.0, ((0, 2), (1, 4), (2, 4)), jnp.float32),
        "rcv_cur": centred(keys[4], (SHOTS, NX, NY, NZ), 1.0, 6.0, ((0, 2), (1, 4), (2, 4)), jnp.float32),
        "src_pos": jax.random.randint(keys[5], (SHOTS,), 0, NX * NY * NZ).astype(jnp.int32),
        "src_amp": centred(keys[6], (SHOTS, STEPS), 4.0, 24.0, ((0, 2),), jnp.float32),
        "rcv_pos": plant(jax.random.randint(keys[7], (SHOTS, RCV), 0, NX * NY * NZ), jax.random.fold_in(keys[7], 1), 0, (NX * NY * NZ) - 1).astype(jnp.int32),
        "rcv_data": centred(keys[8], (SHOTS, STEPS, RCV), 2.0, 6.0, ((0, 2),), jnp.float32),
        "aperture": draw_aperture(jax.random.fold_in(keys[11], 71), 0),
        "owner": draw_owner(jax.random.fold_in(keys[11], 71), 0),
    }


LAP_CENTER = -2.5
LAP_NEAR = 4.0 / 3.0
LAP_FAR = -1.0 / 12.0


def laplacian(widened):
    centre = widened[..., 2:-2, 2:-2, :]
    summed = 3.0 * LAP_CENTER * centre
    summed = summed + LAP_NEAR * (widened[..., 3:-1, 2:-2, :] + widened[..., 1:-3, 2:-2, :])
    summed = summed + LAP_FAR * (widened[..., 4:, 2:-2, :] + widened[..., :-4, 2:-2, :])
    summed = summed + LAP_NEAR * (widened[..., 2:-2, 3:-1, :] + widened[..., 2:-2, 1:-3, :])
    summed = summed + LAP_FAR * (widened[..., 2:-2, 4:, :] + widened[..., 2:-2, :-4, :])
    depth_pad = jnp.pad(centre, [(0, 0)] * (centre.ndim - 1) + [(2, 2)])
    summed = summed + LAP_NEAR * (depth_pad[..., 3:-1] + depth_pad[..., 1:-3])
    summed = summed + LAP_FAR * (depth_pad[..., 4:] + depth_pad[..., :-4])
    return summed


def inject_flat(field_in, positions, values):
    flat_field = field_in.reshape(-1).at[positions].add(values)
    return flat_field.reshape(field_in.shape)


def advance(previous, current, vel_coef):
    padded = jnp.pad(current, ((2, 2), (2, 2), (0, 0)))
    return 2.0 * current - previous + vel_coef * laplacian(padded)


def reference(vel_coef, src_prev, src_cur, rcv_prev, rcv_cur, src_pos, src_amp, rcv_pos, rcv_data, aperture, owner):
    tile_numbers = ((jnp.arange(NX) // CX)[:, None] * N_GY + (jnp.arange(NY) // CY)[None, :]).astype(jnp.int32)

    def one_shot(image, shot_items):
        src_old, src_now, rcv_old, rcv_now, src_where, src_wave, rcv_where, rcv_wave, ap_row = shot_items
        cell_mask = jnp.any(tile_numbers[:, :, None] == ap_row[None, None, :], axis=2).astype(jnp.float32)
        snapshots = []
        for step_index in range(STEPS):
            src_new = inject_flat(advance(src_old, src_now, vel_coef), src_where, src_wave[step_index])
            rcv_new = inject_flat(advance(rcv_old, rcv_now, vel_coef), rcv_where, rcv_wave[step_index])
            src_old, src_now = src_now, src_new
            rcv_old, rcv_now = rcv_now, rcv_new
            snapshots.append((jnp.pad(src_now, ((HALF, HALF), (0, 0), (0, 0))), jnp.pad(rcv_now, ((HALF, HALF), (0, 0), (0, 0)))))
        offset_rows = []
        for offset_index in range(OFFS):
            lead_start = 2 * HALF - offset_index
            summed = None
            for src_ext, rcv_ext in snapshots:
                product_term = src_ext[lead_start:lead_start + NX] * rcv_ext[offset_index:offset_index + NX]
                summed = product_term if summed is None else summed + product_term
            offset_rows.append(summed)
        contribution = jnp.stack(offset_rows) * cell_mask[None, :, :, None]
        return image + contribution, (src_now, rcv_now)

    image_start = jnp.zeros((OFFS, NX, NY, NZ), jnp.float32)
    image, (src_next, rcv_next) = lax.scan(one_shot, image_start, (src_prev, src_cur, rcv_prev, rcv_cur, src_pos, src_amp, rcv_pos, rcv_data, aperture))
    strips = image.reshape(OFFS, N_GX, NT, SX, N_GY, CY, NZ)
    strips = jnp.transpose(strips, (1, 4, 2, 0, 3, 5, 6)).reshape(NT, NT, OFFS, SX, CY, NZ)
    matches = owner[:, :, None] == jnp.arange(NT, dtype=jnp.int32)[None, None, :]
    strip_for = jnp.sum(jnp.where(matches, jnp.arange(NT, dtype=jnp.int32)[None, :, None], 0), axis=1).astype(jnp.int32)
    picked = jax.vmap(lambda tile_strips, tile_index: jnp.take(tile_strips, tile_index, axis=0))(strips, strip_for)
    gathers = jnp.transpose(picked, (1, 2, 0, 3, 4, 5))
    return src_next, rcv_next, gathers
```

```python
import functools

import jax
import jax.numpy as jnp
from jax import lax
from jax.experimental import pallas as pl
from jax.experimental.pallas import tpu as pltpu
from jax.sharding import PartitionSpec as P

OFFS = 16
STEPS = 3
HALF = 8
PAD = 8
VALID = (6, 4, 2)
CORNER = 6

LAP_CENTER = -2.5
LAP_NEAR = 4.0 / 3.0
LAP_FAR = -1.0 / 12.0

ANY = pl.BlockSpec(memory_space=pl.ANY)
SMEM = pl.BlockSpec(memory_space=pltpu.SMEM)
VMEM = pl.BlockSpec(memory_space=pltpu.VMEM)


def swap_pairs(count):
    first = [(i, i ^ 1) for i in range(count) if (i ^ 1) < count]
    second = []
    for i in range(1, count - 1, 2):
        second += [(i, i + 1), (i + 1, i)]
    return first, second


def largest_block(count, limit):
    return max(n for n in range(1, limit + 1) if count % n == 0)


def run_copies(copies):
    for copy in copies:
        copy.start()
    for copy in copies:
        copy.wait()


def is_upper(axis, swap):
    return lax.rem(lax.axis_index(axis) + swap, 2) == 0


def pick(condition, upper, lower, multiple=1):
    return pl.multiple_of(jnp.where(condition, upper, lower), multiple)


def pack_kernel(vel, src_prev, src_cur, rcv_prev, rcv_cur, x0, x1, y0, y1, sems):
    width_x, width_y, depth = vel.shape
    fields = (src_cur.at[0], rcv_cur.at[0], src_prev.at[0], rcv_prev.at[0], vel)
    copies = []

    def add(src, dst):
        copies.append(pltpu.make_async_copy(src, dst, sems.at[len(copies)]))

    for swap, out in enumerate((y0, y1)):
        start = pick(is_upper("gy", swap), width_y - PAD, 0, PAD)
        for n, field in enumerate(fields):
            add(field.at[:, pl.ds(start, PAD)], out.at[n])
    for swap, out in enumerate((x0, x1)):
        row = 0
        for n, field in enumerate(fields):
            rows = HALF if n < 2 else VALID[0]
            start = pick(is_upper("gx", swap), width_x - rows, 0)
            add(field.at[pl.ds(start, rows)], out.at[pl.ds(row, rows)])
            row += rows
    run_copies(copies)


def corner_kernel(y0, y1, late, c0, c1, sems):
    width_x = y0.shape[1]
    copies = []
    for swap, out in enumerate((c0, c1)):
        start = pick(is_upper("gx", swap), width_x - CORNER, 0)
        for n, halo in enumerate((y0, y1)):
            copies.append(
                pltpu.make_async_copy(halo.at[:, pl.ds(start, CORNER)], out.at[n], sems.at[len(copies)])
            )
    run_copies(copies)


def locate(position, width_x, width_y, depth):
    grid_y = width_y * lax.axis_size("gy")
    x = lax.div(position, grid_y * depth) - lax.axis_index("gx") * width_x
    y = lax.rem(lax.div(position, depth), grid_y) - lax.axis_index("gy") * width_y
    reach = VALID[0]
    inside = (x >= -reach) & (x < width_x + reach) & (y >= -PAD // 2) & (y < width_y + PAD // 2)
    return x, y, lax.rem(position, depth), inside


def spread_kernel(width_x, width_y, positions, values, out):
    rows, depth = out.shape[1], out.shape[2]
    receivers = positions.shape[1]
    x, y, depths, inside = locate(positions[...], width_x, width_y, depth)
    cell_row = jnp.where(inside, (x + VALID[0]) * (width_y + PAD) + y + PAD // 2, -1)
    lanes = lax.broadcasted_iota(jnp.int32, (depth, receivers), 0)
    rest = jnp.concatenate(
        [
            jnp.where(lanes == depths, values[:, t * receivers : (t + 1) * receivers], 0.0)
            for t in range(STEPS)
        ],
        axis=0,
    )
    parts = []
    for _ in range(3):
        parts.append(rest.astype(jnp.bfloat16))
        rest = rest - parts[-1].astype(jnp.float32)
    index = lax.broadcasted_iota(jnp.int32, (rows, receivers), 0)
    hot = jnp.where(index == cell_row, 1.0, 0.0).astype(jnp.bfloat16)
    total = lax.dot_general(
        hot, jnp.concatenate(parts, axis=0), (((1,), (1,)), ((), ())), preferred_element_type=jnp.float32
    )
    for t in range(STEPS):
        high, middle, low = (
            total[:, (n * STEPS + t) * depth : (n * STEPS + t + 1) * depth] for n in range(3)
        )
        out[t] = high + (middle + low)


def depth_matrix(depth):
    row = lax.broadcasted_iota(jnp.int32, (depth, depth), 0)
    col = lax.broadcasted_iota(jnp.int32, (depth, depth), 1)
    apart = jnp.abs(row - col)
    return jnp.where(apart == 1, 16.0, jnp.where(apart == 2, -1.0, 0.0)).astype(jnp.bfloat16)


def depth_neighbours(here, matrix):
    rest = here.reshape(-1, here.shape[-1])
    total = None
    for _ in range(3):
        part = rest.astype(jnp.bfloat16)
        rest = rest - part.astype(jnp.float32)
        term = jnp.dot(part, matrix, preferred_element_type=jnp.float32)
        total = term if total is None else total + term
    return total.reshape(here.shape)


def advance(cur, prev, vel, out, inject, rows, cols, matrix):
    first, count = rows
    col, width = cols
    block = largest_block(count, 22)

    def one(step, carry):
        x = first + step * block
        at = lambda ref, dx, dy: ref[pl.ds(x + dx, block), pl.ds(col + dy, width), :]
        here = at(cur, 0, 0)
        near = at(cur, 1, 0) + at(cur, -1, 0) + at(cur, 0, 1) + at(cur, 0, -1)
        far = at(cur, 2, 0) + at(cur, -2, 0) + at(cur, 0, 2) + at(cur, 0, -2)
        lap = (3.0 * LAP_CENTER) * here + LAP_NEAR * near + LAP_FAR * far
        lap = lap + (1.0 / 12.0) * depth_neighbours(here, matrix)
        new = 2.0 * here - at(prev, 0, 0) + at(vel, 0, 0) * lap
        if inject is not None:
            new = new + inject[pl.ds(x - (PAD - VALID[0]), block), pl.ds(col - PAD // 2, width), :]
        out[pl.ds(x, block), pl.ds(col, width), :] = new
        return carry

    lax.fori_loop(0, count // block, one, 0)


def chunk_shift(i, r):
    shots = lax.axis_size("shot")
    held = OFFS // shots
    keeper = lax.rem(lax.axis_index("shot") + r, shots)
    return HALF - (keeper * held + jnp.where(2 * keeper < shots, held - 1 - i, i))


def read_tables(owner, aperture, strip_for):
    tile = lax.axis_index(("gx", "gy"))
    for k in range(owner.shape[0]):
        strip_for[owner[tile, k]] = k
    active = aperture[0, 0] == tile
    for k in range(1, aperture.shape[1]):
        active = active | (aperture[0, k] == tile)
    return active


def correlate(lead, lag, strip_for, keep, tiles, strip_rows, cols, outs, slot, i):
    shifts = [chunk_shift(i, r) for r in range(len(outs))]

    def one(tile, carry):
        for u in range(strip_rows):
            x = HALF + strip_for[tile] * strip_rows + u
            for r, out in enumerate(outs):
                shift = shifts[r]
                total = None
                for t in range(STEPS):
                    term = lead(t, x + shift, cols) * lag(t, x - shift, cols)
                    total = term if total is None else total + term
                out[tile, slot, u] = jnp.where(keep, total, 0.0)
        return carry

    lax.fori_loop(0, tiles, one, 0)


def front_kernel(
    early, shots, tiles, owner, aperture, src_pos, amps,
    vel, src_prev, src_cur, rcv_prev, rcv_cur, x0, x1, y0, y1, c0, c1, inject_hbm, *rest
):
    count = shots if early else 0
    outs = rest[:count]
    src_next, rcv_next, snaps, edge0, edge1 = rest[count : count + 5]
    ext, s1, s2, s3, inject, strip_for, in_sems, out_sems = rest[count + 5 :]
    width_x, width_y, depth = vel.shape
    inner_y = pl.ds(PAD, width_y)
    copies = []

    def add(src, dst):
        copies.append(pltpu.make_async_copy(src, dst, in_sems.at[len(copies)]))

    for n, field in enumerate((src_cur.at[0], rcv_cur.at[0], src_prev.at[0], rcv_prev.at[0], vel)):
        add(field, ext.at[n, pl.ds(PAD, width_x), inner_y])
    for swap, halo in enumerate((y0, y1)):
        col = pick(is_upper("gy", swap), PAD + width_y, 0, PAD)
        add(halo, ext.at[:, pl.ds(PAD, width_x), pl.ds(col, PAD)])
    for swap, halo in enumerate((x0, x1)):
        row = 0
        for n in range(5):
            rows = HALF if n < 2 else VALID[0]
            start = pick(is_upper("gx", swap), PAD + width_x, PAD - rows)
            add(halo.at[pl.ds(row, rows)], ext.at[n, pl.ds(start, rows), inner_y])
            row += rows
    for swap, corner in enumerate((c0, c1)):
        start = pick(is_upper("gx", swap), PAD + width_x, PAD - CORNER)
        for n in range(2):
            col = pick(is_upper("gy", n), PAD + width_y, 0, PAD)
            add(corner.at[n], ext.at[:, pl.ds(start, CORNER), pl.ds(col, PAD)])
    add(inject_hbm, inject)
    for copy in copies:
        copy.start()
    for copy in copies[:-1]:
        copy.wait()

    lane = lax.broadcasted_iota(jnp.int32, (1, depth), 1)
    matrix = depth_matrix(depth)
    fields = [(ext.at[0], ext.at[1])] + [(s.at[0], s.at[1]) for s in (s1, s2, s3)]
    before = (ext.at[2], ext.at[3])
    src_x, src_y, src_z, src_here = locate(src_pos[0], width_x, width_y, depth)
    src_x = jnp.where(src_here, src_x + PAD, PAD)
    src_y = jnp.where(src_here, src_y + PAD, PAD)
    keep = read_tables(owner, aperture, strip_for)
    sends = []

    def send(src, dst):
        copy = pltpu.make_async_copy(src, dst, out_sems.at[len(sends)])
        copy.start()
        sends.append(copy)

    for f in range(2):
        if f == 1:
            copies[-1].wait()
        for t in range(STEPS):
            reach = VALID[t]
            rows = (PAD - reach, width_x + 2 * reach)
            cols = (PAD, width_y) if t == STEPS - 1 else (PAD // 2, width_y + PAD)
            prev = before[f] if t == 0 else fields[t - 1][f]
            out = fields[t + 1][f]
            advance(
                fields[t][f], prev, ext.at[4], out, inject.at[t] if f == 1 else None, rows, cols, matrix
            )
            if f == 0:

                @pl.when(src_here)
                def _():
                    row = out[src_x, pl.ds(src_y, 1), :]
                    out[src_x, pl.ds(src_y, 1), :] = row + jnp.where(lane == src_z, amps[0, t], 0.0)

            send(out.at[pl.ds(PAD - reach, width_x + 2 * reach), inner_y],
                 snaps.at[t, f, pl.ds(PAD - reach, width_x + 2 * reach)])
            if t == STEPS - 1:
                send(out.at[pl.ds(PAD, width_x), inner_y], (src_next, rcv_next)[f].at[0])
    row = 0
    for t in range(STEPS):
        rows = HALF - VALID[t]
        for f in range(2):
            for swap, edge in enumerate((edge0, edge1)):
                start = pick(is_upper("gx", swap), PAD + width_x - HALF, PAD + VALID[t])
                send(fields[t + 1][f].at[pl.ds(start, rows), inner_y], edge.at[pl.ds(row, rows)])
            row += rows
    strip_rows = width_x // tiles
    for i in range(early):
        correlate(
            lambda t, x, c: fields[t + 1][0][x, c, :],
            lambda t, x, c: fields[t + 1][1][x, c, :],
            strip_for, keep, tiles, strip_rows, inner_y, outs, i, i,
        )
    for copy in sends:
        copy.wait()


def rest_kernel(groups, shots, tiles, owner, aperture, snaps, edge0, edge1, *rest):
    outs = rest[: len(groups) * shots]
    held, strip_for, sems = rest[len(groups) * shots :]
    width_x = held.shape[2] - 2 * HALF
    copies = []

    def add(src, dst):
        copies.append(pltpu.make_async_copy(src, dst, sems.at[len(copies)]))

    row = 0
    for t in range(STEPS):
        reach = VALID[t]
        rows = HALF - reach
        for f in range(2):
            span = pl.ds(HALF - reach, width_x + 2 * reach)
            add(snaps.at[t, f, span], held.at[t, f, span])
            for swap, edge in enumerate((edge0, edge1)):
                start = pick(is_upper("gx", swap), HALF + width_x + reach, 0)
                add(edge.at[pl.ds(row, rows)], held.at[t, f, pl.ds(start, rows)])
            row += rows
    keep = read_tables(owner, aperture, strip_for)
    run_copies(copies)
    for g, group in enumerate(groups):
        for slot, i in enumerate(group):
            correlate(
                lambda t, x, c: held[t, 0, x],
                lambda t, x, c: held[t, 1, x],
                strip_for, keep, tiles, width_x // tiles, None,
                outs[g * shots : (g + 1) * shots], slot, i,
            )


def sum_kernel(*refs):
    total = refs[0][...]
    for part in refs[1:-1]:
        total = total + part[...]
    refs[-1][...] = total


def body(
    vel_coef, src_prev, src_cur, rcv_prev, rcv_cur, src_pos, src_amp, rcv_pos, rcv_data, aperture, owner
):
    f32 = jnp.float32
    width_x, width_y, depth = vel_coef.shape
    n_gx, n_gy, shots = lax.axis_size("gx"), lax.axis_size("gy"), lax.axis_size("shot")
    tiles = n_gx * n_gy
    strip_rows = width_x // tiles
    shot = lax.axis_index("shot")
    swaps_x, swaps_y = swap_pairs(n_gx), swap_pairs(n_gy)

    held = OFFS // shots
    chunk_offset = [
        [o * held + (held - 1 - i if 2 * o < shots else i) for o in range(shots)] for i in range(held)
    ]
    early = 0
    while early < held and all(abs(HALF - h) <= VALID[-1] for h in chunk_offset[early]):
        early += 1
    ext_x, ext_y = width_x + 2 * VALID[0], width_y + PAD

    big = pltpu.CompilerParams(vmem_limit_bytes=60 * 1024 * 1024)
    x_rows = 2 * HALF + 3 * VALID[0]
    args = (vel_coef, src_prev, src_cur, rcv_prev, rcv_cur)

    x_part = jax.ShapeDtypeStruct((x_rows, width_y, depth), f32)
    y_part = jax.ShapeDtypeStruct((5, width_x, PAD, depth), f32)
    sends = pl.pallas_call(
        pack_kernel,
        out_shape=(x_part, x_part, y_part, y_part),
        in_specs=[ANY] * 5,
        out_specs=(VMEM,) * 4,
        scratch_shapes=[pltpu.SemaphoreType.DMA((20,))],
        compiler_params=big,
        name="pack_halos",
    )(*args)
    halos = [lax.ppermute(sends[n], "gx", swaps_x[n]) for n in range(2)]
    halos += [lax.ppermute(sends[2 + n], "gy", swaps_y[n]) for n in range(2)]

    receivers = rcv_pos.shape[1]
    inject = pl.pallas_call(
        functools.partial(spread_kernel, width_x, width_y),
        out_shape=jax.ShapeDtypeStruct((STEPS, ext_x * ext_y, depth), f32),
        in_specs=[VMEM] * 2,
        out_specs=VMEM,
        compiler_params=big,
        cost_estimate=pl.CostEstimate(
            flops=6 * ext_x * ext_y * receivers * depth * STEPS, bytes_accessed=4 * STEPS * ext_x * ext_y * depth,
            transcendentals=0),
        name="spread_receivers",
    )(rcv_pos, rcv_data.reshape(1, STEPS * receivers))
    inject = inject.reshape(STEPS, ext_x, ext_y, depth)

    corner = jax.ShapeDtypeStruct((2, 5, CORNER, PAD, depth), f32)
    corners = pl.pallas_call(
        corner_kernel,
        out_shape=(corner, corner),
        in_specs=[ANY] * 3,
        out_specs=(VMEM, VMEM),
        scratch_shapes=[pltpu.SemaphoreType.DMA((4,))],
        compiler_params=big,
        name="pack_corners",
    )(halos[2], halos[3], inject)
    halos += [lax.ppermute(corners[n], "gx", swaps_x[n]) for n in range(2)]

    def piece(group):
        return jax.ShapeDtypeStruct((tiles, len(group), strip_rows, width_y, depth), f32)

    groups = ([tuple(range(early))] if early else []) + [
        tuple(range(i, min(i + 3, held))) for i in range(early, held, 3)
    ]
    ahead, later = (groups[:1], groups[1:]) if early else ([], groups)
    field = jax.ShapeDtypeStruct(src_cur.shape, f32)
    edge_rows = 2 * sum(HALF - v for v in VALID)
    edge = jax.ShapeDtypeStruct((edge_rows, width_y, depth), f32)
    snap_shape = (STEPS, 2, width_x + 2 * HALF, width_y, depth)
    span = (width_x + 2 * PAD, width_y + 2 * PAD, depth)
    step_ops = 60 * width_x * width_y * depth * STEPS
    result = pl.pallas_call(
        functools.partial(front_kernel, early, shots, tiles),
        out_shape=tuple(piece(g) for g in ahead) * shots
        + (field, field, jax.ShapeDtypeStruct(snap_shape, f32), edge, edge),
        in_specs=[SMEM] * 4 + [ANY] * 12,
        out_specs=(VMEM,) * (len(ahead) * shots) + (ANY,) * 5,
        scratch_shapes=[
            pltpu.VMEM((5,) + span, f32),
            pltpu.VMEM((2,) + span, f32),
            pltpu.VMEM((2,) + span, f32),
            pltpu.VMEM((2,) + span, f32),
            pltpu.VMEM((STEPS, ext_x, ext_y, depth), f32),
            pltpu.SMEM((tiles,), jnp.int32),
            pltpu.SemaphoreType.DMA((22,)),
            pltpu.SemaphoreType.DMA((20,)),
        ],
        compiler_params=big,
        cost_estimate=pl.CostEstimate(flops=step_ops, bytes_accessed=12 * 2**20, transcendentals=0),
        name="three_steps",
    )(owner, aperture, src_pos, src_amp, *args, *halos, inject)
    pieces = list(result[: len(ahead) * shots])
    src_next, rcv_next, snaps, *edges = result[len(ahead) * shots :]
    edges = [lax.ppermute(edges[n], "gx", swaps_x[n]) for n in range(2)]
    if later:
        pieces += pl.pallas_call(
            functools.partial(rest_kernel, later, shots, tiles),
            out_shape=tuple(piece(g) for g in later for _ in range(shots)),
            in_specs=[SMEM] * 2 + [ANY] * 3,
            out_specs=(VMEM,) * (len(later) * shots),
            scratch_shapes=[
                pltpu.VMEM(snap_shape, f32), pltpu.SMEM((tiles,), jnp.int32), pltpu.SemaphoreType.DMA((18,))],
            compiler_params=big,
            cost_estimate=pl.CostEstimate(
                flops=5 * OFFS * width_x * width_y * depth, bytes_accessed=12 * 2**20, transcendentals=0),
            name="other_offsets",
        )(owner, aperture, snaps, *edges)

    gathers = jnp.zeros((1, held, tiles, strip_rows, width_y, depth), f32)
    for g, group in enumerate(groups):
        going = pieces[g * shots + 1 : (g + 1) * shots]
        if g >= 2:
            going, coming = lax.optimization_barrier((going, coming))
        coming = [
            lax.ppermute(cells, "shot", [(s, (s + r + 1) % shots) for s in range(shots)])
            for r, cells in enumerate(going)
        ]
        parts = [pieces[g * shots]] + coming
        shape = parts[0].shape
        spec = pl.BlockSpec((4,) + shape[1:], lambda n: (n, 0, 0, 0, 0))
        total = pl.pallas_call(
            sum_kernel,
            grid=(tiles // 4,),
            out_shape=jax.ShapeDtypeStruct(shape, f32),
            in_specs=[spec] * shots,
            out_specs=spec,
            compiler_params=pltpu.CompilerParams(vmem_limit_bytes=16 * 1024 * 1024),
            cost_estimate=pl.CostEstimate(flops=2**37, bytes_accessed=2**28, transcendentals=0),
            name="sum_shots",
        )(*parts)
        arrived = lax.all_to_all(total, ("gx", "gy"), split_axis=0, concat_axis=0, tiled=True)
        for slot, i in enumerate(group):
            where = jnp.where(2 * shot < shots, held - 1 - i, i)
            gathers = lax.dynamic_update_slice(gathers, arrived[None, None, :, slot], (0, where, 0, 0, 0, 0))
    return src_next, rcv_next, gathers


def solution(mesh):
    return jax.shard_map(
        body,
        mesh=mesh,
        in_specs=(
            P("gx", "gy", None),
            P("shot", "gx", "gy", None),
            P("shot", "gx", "gy", None),
            P("shot", "gx", "gy", None),
            P("shot", "gx", "gy", None),
            P("shot"),
            P("shot", None),
            P("shot", None),
            P("shot", None, None),
            P("shot", None),
            P(),
        ),
        out_specs=(
            P("shot", "gx", "gy", None),
            P("shot", "gx", "gy", None),
            P(("gx", "gy"), "shot", None, None, None, None),
        ),
        check_vma=False,
    )
```

```python
import functools

import jax
import jax.numpy as jnp
from jax import lax
from jax.experimental import pallas as pl
from jax.experimental.pallas import tpu as pltpu
from jax.sharding import PartitionSpec as P

OFFS = 16
STEPS = 3
HALF = 8
PAD = 8
VALID = (6, 4, 2)
CORNER = 6

LAP_CENTER = -2.5
LAP_NEAR = 4.0 / 3.0
LAP_FAR = -1.0 / 12.0

ANY = pl.BlockSpec(memory_space=pl.ANY)
SMEM = pl.BlockSpec(memory_space=pltpu.SMEM)
VMEM = pl.BlockSpec(memory_space=pltpu.VMEM)


def swap_pairs(count):
    first = [(i, i ^ 1) for i in range(count) if (i ^ 1) < count]
    second = []
    for i in range(1, count - 1, 2):
        second += [(i, i + 1), (i + 1, i)]
    return first, second


def largest_block(count, limit):
    return max(n for n in range(1, limit + 1) if count % n == 0)


def run_copies(copies):
    for copy in copies:
        copy.start()
    for copy in copies:
        copy.wait()


def is_upper(axis, swap):
    return lax.rem(lax.axis_index(axis) + swap, 2) == 0


def pick(condition, upper, lower, multiple=1):
    return pl.multiple_of(jnp.where(condition, upper, lower), multiple)


def pack_kernel(vel, src_prev, src_cur, rcv_prev, rcv_cur, x0, x1, y0, y1, *scratch):
    *buffers, sems, out_sems = scratch
    width_x, width_y, depth = vel.shape
    fields = (src_cur.at[0], rcv_cur.at[0], src_prev.at[0], rcv_prev.at[0], vel)
    jobs = []
    count = 0
    for swap in range(2):
        start = pick(is_upper("gy", swap), width_y - PAD, 0, PAD)
        copies = []
        for n, field in enumerate(fields):
            copies.append(
                pltpu.make_async_copy(field.at[:, pl.ds(start, PAD)], buffers[2 + swap].at[n], sems.at[count])
            )
            count += 1
        jobs.append((copies, buffers[2 + swap], (y0, y1)[swap]))
    for swap in range(2):
        row = 0
        copies = []
        for n, field in enumerate(fields):
            rows = HALF if n < 2 else VALID[0]
            start = pick(is_upper("gx", swap), width_x - rows, 0)
            copies.append(
                pltpu.make_async_copy(
                    field.at[pl.ds(start, rows)], buffers[swap].at[pl.ds(row, rows)], sems.at[count])
            )
            row += rows
            count += 1
        jobs.append((copies, buffers[swap], (x0, x1)[swap]))
    for copies, _, _ in jobs:
        for copy in copies:
            copy.start()
    sends = []
    for n, (copies, buffer, out) in enumerate(jobs):
        for copy in copies:
            copy.wait()
        sends.append(pltpu.make_async_copy(buffer, out, out_sems.at[n]))
        sends[-1].start()
    for copy in sends:
        copy.wait()


def corner_kernel(y0, y1, late, c0, c1, sems):
    width_x = y0.shape[1]
    copies = []
    for swap, out in enumerate((c0, c1)):
        start = pick(is_upper("gx", swap), width_x - CORNER, 0)
        for n, halo in enumerate((y0, y1)):
            copies.append(
                pltpu.make_async_copy(halo.at[:, pl.ds(start, CORNER)], out.at[n], sems.at[len(copies)])
            )
    run_copies(copies)


def locate(position, width_x, width_y, depth):
    grid_y = width_y * lax.axis_size("gy")
    x = lax.div(position, grid_y * depth) - lax.axis_index("gx") * width_x
    y = lax.rem(lax.div(position, depth), grid_y) - lax.axis_index("gy") * width_y
    reach = VALID[0]
    inside = (x >= -reach) & (x < width_x + reach) & (y >= -PAD // 2) & (y < width_y + PAD // 2)
    return x, y, lax.rem(position, depth), inside


def spread_kernel(width_x, width_y, positions, values, out):
    rows, depth = out.shape[1], out.shape[2]
    receivers = positions.shape[1]
    x, y, depths, inside = locate(positions[...], width_x, width_y, depth)
    cell_row = jnp.where(inside, (x + VALID[0]) * (width_y + PAD) + y + PAD // 2, -1)
    lanes = lax.broadcasted_iota(jnp.int32, (depth, receivers), 0)
    rest = jnp.concatenate(
        [
            jnp.where(lanes == depths, values[:, t * receivers : (t + 1) * receivers], 0.0)
            for t in range(STEPS)
        ],
        axis=0,
    )
    parts = []
    for _ in range(3):
        parts.append(rest.astype(jnp.bfloat16))
        rest = rest - parts[-1].astype(jnp.float32)
    index = lax.broadcasted_iota(jnp.int32, (rows, receivers), 0)
    hot = jnp.where(index == cell_row, 1.0, 0.0).astype(jnp.bfloat16)
    total = lax.dot_general(
        hot, jnp.concatenate(parts, axis=0), (((1,), (1,)), ((), ())), preferred_element_type=jnp.float32
    )
    for t in range(STEPS):
        high, middle, low = (
            total[:, (n * STEPS + t) * depth : (n * STEPS + t + 1) * depth] for n in range(3)
        )
        out[t] = high + (middle + low)


def depth_matrix(depth):
    row = lax.broadcasted_iota(jnp.int32, (depth, depth), 0)
    col = lax.broadcasted_iota(jnp.int32, (depth, depth), 1)
    apart = jnp.abs(row - col)
    return jnp.where(apart == 1, 16.0, jnp.where(apart == 2, -1.0, 0.0)).astype(jnp.bfloat16)


def depth_neighbours(here, matrix):
    rest = here.reshape(-1, here.shape[-1])
    total = None
    for _ in range(3):
        part = rest.astype(jnp.bfloat16)
        rest = rest - part.astype(jnp.float32)
        term = jnp.dot(part, matrix, preferred_element_type=jnp.float32)
        total = term if total is None else total + term
    return total.reshape(here.shape)


def advance(cur, prev, vel, out, inject, rows, cols, matrix):
    first, count = rows
    col, width = cols
    block = largest_block(count, 28)

    def one(step, carry):
        x = first + step * block
        at = lambda ref, dx, dy: ref[pl.ds(x + dx, block), pl.ds(col + dy, width), :]
        here = at(cur, 0, 0)
        near = at(cur, 1, 0) + at(cur, -1, 0) + at(cur, 0, 1) + at(cur, 0, -1)
        far = at(cur, 2, 0) + at(cur, -2, 0) + at(cur, 0, 2) + at(cur, 0, -2)
        lap = (3.0 * LAP_CENTER) * here + LAP_NEAR * near + LAP_FAR * far
        lap = lap + (1.0 / 12.0) * depth_neighbours(here, matrix)
        new = 2.0 * here - at(prev, 0, 0) + at(vel, 0, 0) * lap
        if inject is not None:
            new = new + inject[pl.ds(x - (PAD - VALID[0]), block), pl.ds(col - PAD // 2, width), :]
        out[pl.ds(x, block), pl.ds(col, width), :] = new
        return carry

    if count == block:
        one(0, 0)
    else:
        lax.fori_loop(0, count // block, one, 0)


def chunk_shift(i, r):
    shots = lax.axis_size("shot")
    held = OFFS // shots
    keeper = lax.rem(lax.axis_index("shot") + r, shots)
    return HALF - (keeper * held + jnp.where(2 * keeper < shots, held - 1 - i, i))


def is_active(aperture):
    tile = lax.axis_index(("gx", "gy"))
    active = aperture[0, 0] == tile
    for k in range(1, aperture.shape[1]):
        active = active | (aperture[0, k] == tile)
    return active


def correlate(lead, lag, strips, keep, strip_rows, outs, slot, i):
    shifts = [chunk_shift(i, r) for r in range(len(outs))]
    place, count = strips

    def one(n, carry):
        for u in range(strip_rows):
            x = HALF + place(n) * strip_rows + u
            for r, out in enumerate(outs):
                total = None
                for t in range(STEPS):
                    term = lead(t, x + shifts[r]) * lag(t, x - shifts[r])
                    total = term if total is None else total + term
                out[n, slot, u] = jnp.where(keep, total, 0.0)
        return carry

    lax.fori_loop(0, count, one, 0)


def inner_rows(t, width_x):
    return PAD + 2 * (t + 1), width_x - 4 * (t + 1)


def outer_rows(t, width_x):
    first, count = inner_rows(t, width_x)
    return (PAD - VALID[t], first + VALID[t] - PAD), (first + count, PAD + width_x + VALID[t] - first - count)


def rims(width_x):
    return (PAD + 2, PAD), (width_x - 2, PAD)


class Sources:
    def __init__(self, src_pos, amps, shape):
        width_x, width_y, depth = shape
        x, y, z, here = locate(src_pos[0], width_x, width_y, depth)
        self.row, self.col, self.here, self.amps = x + PAD, y + PAD, here, amps
        self.lane = lax.broadcasted_iota(jnp.int32, (1, depth), 1)
        self.depth = z

    def add(self, out, t, rows):
        first, count = rows

        @pl.when(self.here & (self.row >= first) & (self.row < first + count))
        def _():
            cells = out[self.row, pl.ds(self.col, 1), :]
            out[self.row, pl.ds(self.col, 1), :] = cells + jnp.where(self.lane == self.depth, self.amps[0, t], 0.0)


def column_window(t, width_y):
    return (PAD, width_y) if t == STEPS - 1 else (PAD // 2, width_y + PAD)


def inner_kernel(
    early, shots, owner, aperture, src_pos, amps,
    vel, src_prev, src_cur, rcv_prev, rcv_cur, y0, y1, inject_from, *rest
):
    count = shots if early else 0
    outs, (s1, s2, s3, ext, inject, sems) = rest[:count], rest[count:]
    width_x, width_y, depth = vel.shape
    inner_y = pl.ds(PAD, width_y)
    copies = []

    def add(src, dst):
        copies.append(pltpu.make_async_copy(src, dst, sems.at[len(copies)]))

    for swap, halo in enumerate((y0, y1)):
        col = pick(is_upper("gy", swap), PAD + width_y, 0, PAD)
        add(halo, ext.at[:, pl.ds(PAD, width_x), pl.ds(col, PAD)])
    for n, field in ((0, src_cur.at[0]), (2, src_prev.at[0]), (4, vel), (1, rcv_cur.at[0]), (3, rcv_prev.at[0])):
        add(field, ext.at[n, pl.ds(PAD, width_x), inner_y])
    used = pl.ds(PAD, width_x - 4)
    add(inject_from.at[:, used], inject.at[:, used])
    for copy in copies:
        copy.start()
    keep = is_active(aperture)
    matrix = depth_matrix(depth)
    source = Sources(src_pos, amps, vel.shape)
    for f in range(2):
        for copy in copies[5:] if f else copies[:5]:
            copy.wait()
        fields = [ext.at[f], s1.at[f], s2.at[f], s3.at[f]]
        for t in range(STEPS):
            prev = ext.at[2 + f] if t == 0 else fields[t - 1]
            rows = inner_rows(t, width_x)
            advance(
                fields[t], prev, ext.at[4], fields[t + 1], inject.at[t] if f == 1 else None,
                rows, column_window(t, width_y), matrix,
            )
            if f == 0:
                source.add(fields[t + 1], t, rows)
    steps = (s1, s2, s3)
    strip_rows = width_x // owner.shape[0]
    for i in range(early):
        correlate(
            lambda t, x: steps[t][0, x, inner_y, :], lambda t, x: steps[t][1, x, inner_y, :],
            strip_map(0, width_x, strip_rows), keep, strip_rows, outs, i, i,
        )


def outer_kernel(
    early, shots, owner, aperture, src_pos, amps,
    vel, src_prev, src_cur, rcv_prev, rcv_cur, x0, x1, y0, y1, c0, c1, inject_from, i1, i2, i3, *rest
):
    count = shots if early else 0
    outs, (s1, s2, s3, edge0, edge1, ext, inject, sems, out_sems) = rest[:count], rest[count:]
    width_x, width_y, depth = vel.shape
    inner_y = pl.ds(PAD, width_y)
    copies = []

    def add(src, dst):
        copies.append(pltpu.make_async_copy(src, dst, sems.at[len(copies)]))

    for swap, halo in enumerate((y0, y1)):
        col = pick(is_upper("gy", swap), PAD + width_y, 0, PAD)
        for first in (0, width_x - PAD):
            add(halo.at[:, pl.ds(first, PAD)], ext.at[:, pl.ds(PAD + first, PAD), pl.ds(col, PAD)])
    for swap, corner in enumerate((c0, c1)):
        start = pick(is_upper("gx", swap), PAD + width_x, PAD - CORNER)
        for n in range(2):
            col = pick(is_upper("gy", n), PAD + width_y, 0, PAD)
            add(corner.at[n], ext.at[:, pl.ds(start, CORNER), pl.ds(col, PAD)])
    row = 0
    fields = (src_cur.at[0], rcv_cur.at[0], src_prev.at[0], rcv_prev.at[0], vel)
    for n in range(5):
        rows = HALF if n < 2 else VALID[0]
        for swap, halo in enumerate((x0, x1)):
            start = pick(is_upper("gx", swap), PAD + width_x, PAD - rows)
            add(halo.at[pl.ds(row, rows)], ext.at[n, pl.ds(start, rows), inner_y])
        for first in (0, width_x - PAD):
            add(fields[n].at[pl.ds(first, PAD)], ext.at[n, pl.ds(PAD + first, PAD), inner_y])
        row += rows
    for first, rows in rims(width_x):
        for inner, step in ((i1, s1), (i2, s2), (i3, s3)):
            add(inner.at[:, pl.ds(first, rows)], step.at[:, pl.ds(first, rows)])
    for first in (0, inject.shape[1] - 12):
        used = pl.ds(first, 12)
        add(inject_from.at[:, used], inject.at[:, used])
    for copy in copies:
        copy.start()
    keep = is_active(aperture)
    matrix = depth_matrix(depth)
    source = Sources(src_pos, amps, vel.shape)
    for copy in copies:
        copy.wait()
    chain = [[ext.at[f], s1.at[f], s2.at[f], s3.at[f]] for f in range(2)]
    for t in range(STEPS):
        for f, fields in enumerate(chain):
            prev = ext.at[2 + f] if t == 0 else fields[t - 1]
            for rows in outer_rows(t, width_x):
                advance(
                    fields[t], prev, ext.at[4], fields[t + 1], inject.at[t] if f == 1 else None,
                    rows, column_window(t, width_y), matrix,
                )
        for rows in outer_rows(t, width_x):
            source.add(chain[0][t + 1], t, rows)
    steps = (s1, s2, s3)
    sends = []
    row = 0
    for t in range(STEPS):
        rows = HALF - VALID[t]
        for f in range(2):
            for swap, edge in enumerate((edge0, edge1)):
                start = pick(is_upper("gx", swap), PAD + width_x - HALF, PAD + VALID[t])
                sends.append(
                    pltpu.make_async_copy(
                        steps[t].at[f, pl.ds(start, rows), inner_y], edge.at[pl.ds(row, rows)],
                        out_sems.at[len(sends)],
                    )
                )
                sends[-1].start()
            row += rows
    strip_rows = width_x // owner.shape[0]
    for i in range(early):
        correlate(
            lambda t, x: steps[t][0, x, inner_y, :], lambda t, x: steps[t][1, x, inner_y, :],
            strip_map(1, width_x, strip_rows), keep, strip_rows, outs, i, i,
        )
    for copy in sends:
        copy.wait()


def strip_map(part, width_x, strip_rows):
    side = HALF // strip_rows
    middle = (width_x - 2 * HALF) // strip_rows
    if part == 0:
        return lambda n: n + side, middle
    return lambda n: n + jnp.where(n < side, 0, middle), 2 * side


def rest_kernel(part, groups, shots, owner, aperture, i1, i2, i3, o1, o2, o3, *rest):
    edges, rest = rest[: 3 * part], rest[3 * part :]
    count = len(groups) * shots
    results, rest = rest[:count], rest[count:]
    last, rest = rest[: 2 - 2 * part], rest[2 - 2 * part :]
    outs, (held, sems, out_sems) = (results[0], *rest[: count - 1]), rest[count - 1 :]
    width_x = held.shape[2] - 2 * HALF
    inner_y = pl.ds(PAD, held.shape[3])
    copies = []

    def add(src, dst):
        copies.append(pltpu.make_async_copy(src, dst, sems.at[len(copies)]))

    (low, rim), (high, _) = rims(width_x)
    row = 0
    for t, (inner, outer) in enumerate(((i1, o1), (i2, o2), (i3, o3))):
        reach = VALID[t] if part else 0
        rows = HALF - VALID[t]
        middle = pl.ds(low + rim, high - low - rim)
        spans = (pl.ds(PAD - reach, low + rim - PAD + reach), pl.ds(high, PAD + width_x + reach - high))
        add(inner.at[:, middle, inner_y], held.at[t, :, middle])
        for span in spans:
            add(outer.at[:, span, inner_y], held.at[t, :, span])
        for f in range(2 * part):
            for swap, edge in enumerate(edges[:2]):
                start = pick(is_upper("gx", swap), HALF + width_x + reach, 0)
                add(edge.at[pl.ds(row, rows)], held.at[t, f, pl.ds(start, rows)])
            row += rows
    keep = is_active(aperture)
    run_copies(copies)
    sends = []

    def send(src, dst):
        sends.append(pltpu.make_async_copy(src, dst, out_sems.at[len(sends)]))
        sends[-1].start()

    strip_rows = width_x // owner.shape[0]
    for g, group in enumerate(groups):
        for slot, i in enumerate(group):
            places = slice(g * shots, (g + 1) * shots)
            correlate(
                lambda t, x: held[t, 0, x], lambda t, x: held[t, 1, x],
                strip_map(part, width_x, strip_rows), keep, strip_rows, outs[places], slot, i,
            )
            for out, result in zip(outs[places], results[places]):
                if out is not result:
                    send(out.at[:, slot], result.at[:, slot])
    for f, out in enumerate(last):
        send(held.at[STEPS - 1, f, pl.ds(HALF, width_x)], out.at[0])
    for copy in sends:
        copy.wait()


def sum_kernel(part, shots, owner, *refs):
    parts = refs[:shots]
    total, cells, sems = refs[shots + part :]
    tiles = owner.shape[0]
    tile = lax.axis_index(("gx", "gy"))
    strip, count = strip_map(part, parts[0].shape[2] * tiles, parts[0].shape[2])
    copies = []
    for n in range(count):
        one = parts[0][n]
        for other in parts[1:]:
            one = one + other[n]
        cells[n] = one
        copies.append(pltpu.make_async_copy(cells.at[n], total.at[owner[tile, strip(n)]], sems.at[n]))
        copies[-1].start()
    for copy in copies:
        copy.wait()


def place_kernel(group, held, old, piece, out, sems):
    shots = lax.axis_size("shot")
    copies = []
    for slot, i in enumerate(group):
        where = jnp.where(2 * lax.axis_index("shot") < shots, held - 1 - i, i)
        copies.append(pltpu.make_async_copy(piece.at[:, slot], out.at[0, where], sems.at[slot]))
    run_copies(copies)


def body(
    vel_coef, src_prev, src_cur, rcv_prev, rcv_cur, src_pos, src_amp, rcv_pos, rcv_data, aperture, owner
):
    f32 = jnp.float32
    width_x, width_y, depth = vel_coef.shape
    n_gx, n_gy, shots = lax.axis_size("gx"), lax.axis_size("gy"), lax.axis_size("shot")
    tiles = n_gx * n_gy
    strip_rows = width_x // tiles
    shot = lax.axis_index("shot")
    swaps_x, swaps_y = swap_pairs(n_gx), swap_pairs(n_gy)

    held = OFFS // shots
    chunk_offset = [
        [o * held + (held - 1 - i if 2 * o < shots else i) for o in range(shots)] for i in range(held)
    ]
    early = 0
    while early < held and all(abs(HALF - h) <= VALID[-1] for h in chunk_offset[early]):
        early += 1
    ext_x, ext_y = width_x + 2 * VALID[0], width_y + PAD

    small = pltpu.CompilerParams(vmem_limit_bytes=16 * 1024 * 1024)
    big = pltpu.CompilerParams(vmem_limit_bytes=24 * 1024 * 1024)
    x_rows = 2 * HALF + 3 * VALID[0]
    args = (vel_coef, src_prev, src_cur, rcv_prev, rcv_cur)

    x_part = jax.ShapeDtypeStruct((x_rows, width_y, depth), f32)
    y_part = jax.ShapeDtypeStruct((5, width_x, PAD, depth), f32)
    sends = pl.pallas_call(
        pack_kernel,
        out_shape=(x_part, x_part, y_part, y_part),
        in_specs=[ANY] * 5,
        out_specs=(ANY,) * 4,
        scratch_shapes=[pltpu.VMEM(part.shape, f32) for part in (x_part, x_part, y_part, y_part)]
        + [pltpu.SemaphoreType.DMA((20,)), pltpu.SemaphoreType.DMA((4,))],
        compiler_params=pltpu.CompilerParams(vmem_limit_bytes=60 * 1024 * 1024),
        name="pack_halos",
    )(*args)
    halos = [lax.ppermute(sends[n], "gx", swaps_x[n]) for n in range(2)]
    halos += [lax.ppermute(sends[2 + n], "gy", swaps_y[n]) for n in range(2)]

    receivers = rcv_pos.shape[1]
    inject = pl.pallas_call(
        functools.partial(spread_kernel, width_x, width_y),
        out_shape=jax.ShapeDtypeStruct((STEPS, ext_x * ext_y, depth), f32),
        in_specs=[VMEM] * 2,
        out_specs=VMEM,
        compiler_params=big,
        cost_estimate=pl.CostEstimate(
            flops=6 * ext_x * ext_y * receivers * depth * STEPS, bytes_accessed=4 * STEPS * ext_x * ext_y * depth,
            transcendentals=0),
        name="spread_receivers",
    )(rcv_pos, rcv_data.reshape(1, STEPS * receivers))
    inject = inject.reshape(STEPS, ext_x, ext_y, depth)

    corner = jax.ShapeDtypeStruct((2, 5, CORNER, PAD, depth), f32)
    corners = pl.pallas_call(
        corner_kernel,
        out_shape=(corner, corner),
        in_specs=[ANY] * 3,
        out_specs=(VMEM, VMEM),
        scratch_shapes=[pltpu.SemaphoreType.DMA((4,))],
        compiler_params=big,
        name="pack_corners",
    )(halos[2], halos[3], inject)
    halos += [lax.ppermute(corners[n], "gx", swaps_x[n]) for n in range(2)]

    def piece(strips, group):
        return jax.ShapeDtypeStruct((strips, len(group), strip_rows, width_y, depth), f32)

    first = tuple(range(early))
    groups = [tuple(range(i, min(i + 3, held))) for i in range(early, held, 3)]
    edge_rows = 2 * sum(HALF - v for v in VALID)
    edge = jax.ShapeDtypeStruct((edge_rows, width_y, depth), f32)
    span = (width_x + 2 * PAD, width_y + 2 * PAD, depth)
    step = jax.ShapeDtypeStruct((2,) + span, f32)
    step_ops = 30 * width_x * width_y * depth * STEPS
    tables = (owner, aperture)
    middle = (width_x - 2 * HALF) // strip_rows
    inner = pl.pallas_call(
        functools.partial(inner_kernel, early, shots),
        out_shape=(piece(middle, first),) * (shots if early else 0) + (step,) * 3,
        in_specs=[SMEM] * 4 + [ANY] * 8,
        out_specs=(VMEM,) * ((shots if early else 0) + 3),
        scratch_shapes=[
            pltpu.VMEM((5,) + span, f32),
            pltpu.VMEM((STEPS, ext_x, ext_y, depth), f32),
            pltpu.SemaphoreType.DMA((8,)),
        ],
        compiler_params=big,
        cost_estimate=pl.CostEstimate(flops=step_ops, bytes_accessed=12 * 2**20, transcendentals=0),
        name="inner_steps",
    )(*tables, src_pos, src_amp, *args, *halos[2:4], inject)
    inner_pieces, inner = inner[:-3], inner[-3:]
    outer = pl.pallas_call(
        functools.partial(outer_kernel, early, shots),
        out_shape=(piece(tiles - middle, first),) * (shots if early else 0) + (step,) * 3 + (edge, edge),
        in_specs=[SMEM] * 4 + [ANY] * 15,
        out_specs=(VMEM,) * ((shots if early else 0) + 3) + (VMEM,) * 2,
        scratch_shapes=[
            pltpu.VMEM((5,) + span, f32),
            pltpu.VMEM((STEPS, ext_x, ext_y, depth), f32),
            pltpu.SemaphoreType.DMA((40,)),
            pltpu.SemaphoreType.DMA((12,)),
        ],
        compiler_params=big,
        cost_estimate=pl.CostEstimate(flops=step_ops, bytes_accessed=12 * 2**20, transcendentals=0),
        name="outer_steps",
    )(*tables, src_pos, src_amp, *args, *halos, inject, *inner)
    outer_pieces, outer, edges = outer[:-5], outer[-5:-2], outer[-2:]
    edges = [lax.ppermute(edges[n], "gx", swaps_x[n]) for n in range(2)]
    field = jax.ShapeDtypeStruct(src_cur.shape, f32)

    def others(part, *operands):
        strips = middle if part == 0 else tiles - middle
        shapes = [piece(strips, g).shape for g in groups for _ in range(shots)]
        result = pl.pallas_call(
            functools.partial(rest_kernel, part, groups, shots),
            out_shape=(jax.ShapeDtypeStruct(shapes[0], f32),)
            + tuple(pltpu.HBM(shape, f32) for shape in shapes[1:])
            + (field,) * (2 - 2 * part),
            in_specs=[SMEM] * 2 + [ANY] * len(operands),
            out_specs=(VMEM,) + (ANY,) * (len(shapes) + 1 - 2 * part),
            scratch_shapes=[pltpu.VMEM(shape, f32) for shape in shapes[1:]]
            + [
                pltpu.VMEM((STEPS, 2, width_x + 2 * HALF, width_y, depth), f32),
                pltpu.SemaphoreType.DMA((21,)),
                pltpu.SemaphoreType.DMA((2 + held * shots,)),
            ],
            compiler_params=big,
            cost_estimate=pl.CostEstimate(
                flops=5 * OFFS * width_x * width_y * depth, bytes_accessed=12 * 2**20, transcendentals=0),
            name=("far_strips", "near_strips")[part],
        )(*tables, *operands)
        return result[: len(shapes)], result[len(shapes) :]

    def swapped(cells):
        return [
            lax.ppermute(one, "shot", [(s, (s + r + 1) % shots) for s in range(shots)])
            for r, one in enumerate(cells)
        ]

    long_cost = pl.CostEstimate(flops=2**37, bytes_accessed=2**28, transcendentals=0)

    def summed(kept, coming, group):
        total = []
        for part in range(2):
            cells = list(kept[part]) + list(coming[part])
            total = [
                pl.pallas_call(
                    functools.partial(sum_kernel, part, shots),
                    out_shape=piece(tiles, group),
                    in_specs=[SMEM] + [VMEM] * shots + [ANY] * part,
                    out_specs=ANY,
                    scratch_shapes=[
                        pltpu.VMEM(cells[0].shape, f32), pltpu.SemaphoreType.DMA((cells[0].shape[0],))],
                    input_output_aliases={1 + shots: 0} if part else {},
                    compiler_params=small,
                    cost_estimate=pl.CostEstimate(flops=(2**20, 2**34)[part], bytes_accessed=2**20, transcendentals=0),
                    name=("sum_far", "sum_near")[part],
                )(owner, *cells, *total)
            ]
        return total[0]

    totals = []
    coming = []
    if early:
        both = (inner_pieces, outer_pieces)
        coming = [swapped(cells[1:]) for cells in both]
        totals.append(summed([cells[:1] for cells in both], coming, first))
    far, (src_next, rcv_next) = others(0, *inner, *outer)
    near, _ = others(1, *inner, *outer, *edges, totals[0] if early else edges[0])
    for g, group in enumerate(groups):
        both = [cells[g * shots : (g + 1) * shots] for cells in (far, near)]
        going = [cells[1:] for cells in both]
        if coming:
            if g == 0 and early:
                (going[0], coming) = lax.optimization_barrier((going[0], coming))
            else:
                (going, coming) = lax.optimization_barrier((going, coming))
        coming = [swapped(cells) for cells in going]
        totals.append(summed([cells[:1] for cells in both], coming, group))
    gathers = jnp.zeros((1, held, tiles, strip_rows, width_y, depth), f32)
    chunks = ([first] if early else []) + groups
    for n, (group, total) in enumerate(zip(chunks, totals)):
        arrived = lax.all_to_all(total, ("gx", "gy"), split_axis=0, concat_axis=0, tiled=True)
        if n < len(chunks) - 1:
            for slot, i in enumerate(group):
                where = jnp.where(2 * shot < shots, held - 1 - i, i)
                gathers = lax.dynamic_update_slice(gathers, arrived[None, None, :, slot], (0, where, 0, 0, 0, 0))
            continue
        gathers = pl.pallas_call(
            functools.partial(place_kernel, group, held),
            out_shape=jax.ShapeDtypeStruct(gathers.shape, f32),
            in_specs=[ANY, VMEM],
            out_specs=ANY,
            scratch_shapes=[pltpu.SemaphoreType.DMA((len(group),))],
            input_output_aliases={0: 0},
            compiler_params=small,
            name="place_strips",
        )(gathers, arrived)
    return src_next, rcv_next, gathers


def solution(mesh):
    return jax.shard_map(
        body,
        mesh=mesh,
        in_specs=(
            P("gx", "gy", None),
            P("shot", "gx", "gy", None),
            P("shot", "gx", "gy", None),
            P("shot", "gx", "gy", None),
            P("shot", "gx", "gy", None),
            P("shot"),
            P("shot", None),
            P("shot", None),
            P("shot", None, None),
            P("shot", None),
            P(),
        ),
        out_specs=(
            P("shot", "gx", "gy", None),
            P("shot", "gx", "gy", None),
            P(("gx", "gy"), "shot", None, None, None, None),
        ),
        check_vma=False,
    )
```

```python
import functools

import jax
import jax.numpy as jnp
from jax import lax
from jax.experimental import pallas as pl
from jax.experimental.pallas import tpu as pltpu
from jax.sharding import PartitionSpec as P

OFFS = 16
STEPS = 3
HALF = 8
PAD = 8
VALID = (6, 4, 2)
CORNER = 6

LAP_CENTER = -2.5
LAP_NEAR = 4.0 / 3.0
LAP_FAR = -1.0 / 12.0

ANY = pl.BlockSpec(memory_space=pl.ANY)
SMEM = pl.BlockSpec(memory_space=pltpu.SMEM)
VMEM = pl.BlockSpec(memory_space=pltpu.VMEM)


def swap_pairs(count):
    first = [(i, i ^ 1) for i in range(count) if (i ^ 1) < count]
    second = []
    for i in range(1, count - 1, 2):
        second += [(i, i + 1), (i + 1, i)]
    return first, second


def largest_block(count, limit):
    return max(n for n in range(1, limit + 1) if count % n == 0)


def run_copies(copies):
    for copy in copies:
        copy.start()
    for copy in copies:
        copy.wait()


def is_upper(axis, swap):
    return lax.rem(lax.axis_index(axis) + swap, 2) == 0


def pick(condition, upper, lower, multiple=1):
    return pl.multiple_of(jnp.where(condition, upper, lower), multiple)


Y_PLACES = ((PAD, 0, 0), (PAD, 1, 0), (PAD // 2, 2, 0), (PAD // 2, 2, PAD // 2), (PAD, 3, 0))
Y_TILES = 4


def pack_kernel(
    positions_from, values_from, vel, src_prev, src_cur, rcv_prev, rcv_cur, x0, x1, y0, y1, positions, values, *scratch
):
    *buffers, sems, out_sems = scratch
    small = [
        pltpu.make_async_copy(positions_from, positions, sems.at[20]),
        pltpu.make_async_copy(values_from, values, sems.at[21]),
    ]
    width_x, width_y, depth = vel.shape
    fields = (src_cur.at[0], rcv_cur.at[0], src_prev.at[0], rcv_prev.at[0], vel)
    jobs = []
    count = 0
    for swap in range(2):
        copies = []
        for n, field in enumerate(fields):
            cols, tile, col = Y_PLACES[n]
            start = pick(is_upper("gy", swap), width_y - cols, 0, cols)
            copies.append(
                pltpu.make_async_copy(
                    field.at[:, pl.ds(start, cols)], buffers[2 + swap].at[tile, :, pl.ds(col, cols)],
                    sems.at[count],
                )
            )
            count += 1
        jobs.append((copies, buffers[2 + swap], (y0, y1)[swap]))
    for swap in range(2):
        row = 0
        copies = []
        for n, field in enumerate(fields):
            rows = HALF if n < 2 else VALID[0]
            start = pick(is_upper("gx", swap), width_x - rows, 0)
            copies.append(
                pltpu.make_async_copy(
                    field.at[pl.ds(start, rows)], buffers[swap].at[pl.ds(row, rows)], sems.at[count])
            )
            row += rows
            count += 1
        jobs.append((copies, buffers[swap], (x0, x1)[swap]))
    for copies in [copies for copies, _, _ in jobs] + [small]:
        for copy in copies:
            copy.start()
    sends = []
    for n, (copies, buffer, out) in enumerate(jobs):
        for copy in copies:
            copy.wait()
        sends.append(pltpu.make_async_copy(buffer, out, out_sems.at[n]))
        sends[-1].start()
    for copy in small + sends:
        copy.wait()


def corner_kernel(y0, y1, late, c0, c1, sems):
    width_x = y0.shape[1]
    copies = []
    for swap, out in enumerate((c0, c1)):
        start = pick(is_upper("gx", swap), width_x - CORNER, 0)
        for n, halo in enumerate((y0, y1)):
            copies.append(
                pltpu.make_async_copy(halo.at[:, pl.ds(start, CORNER)], out.at[n], sems.at[len(copies)])
            )
    run_copies(copies)


def locate(position, width_x, width_y, depth):
    grid_y = width_y * lax.axis_size("gy")
    x = lax.div(position, grid_y * depth) - lax.axis_index("gx") * width_x
    y = lax.rem(lax.div(position, depth), grid_y) - lax.axis_index("gy") * width_y
    reach = VALID[0]
    inside = (x >= -reach) & (x < width_x + reach) & (y >= -PAD // 2) & (y < width_y + PAD // 2)
    return x, y, lax.rem(position, depth), inside


def spread_kernel(positions, values, vel, src_prev, src_cur, rcv_prev, rcv_cur, out, ext, sems):
    width_x, width_y, _ = vel.shape
    fields = (src_cur.at[0], rcv_cur.at[0], src_prev.at[0], rcv_prev.at[0], vel)
    others = [
        pltpu.make_async_copy(field, ext.at[n, pl.ds(PAD, width_x), pl.ds(PAD, width_y)], sems.at[n])
        for n, field in enumerate(fields)
    ]
    for copy in others:
        copy.start()
    rows, depth = out.shape[1], out.shape[2]
    receivers = positions.shape[1]
    x, y, depths, inside = locate(positions[...], width_x, width_y, depth)
    cell_row = jnp.where(inside, (x + VALID[0]) * (width_y + PAD) + y + PAD // 2, -1)
    lanes = lax.broadcasted_iota(jnp.int32, (depth, receivers), 0)
    rest = jnp.concatenate(
        [
            jnp.where(lanes == depths, values[:, t * receivers : (t + 1) * receivers], 0.0)
            for t in range(STEPS)
        ],
        axis=0,
    )
    parts = []
    for _ in range(3):
        parts.append(rest.astype(jnp.bfloat16))
        rest = rest - parts[-1].astype(jnp.float32)
    index = lax.broadcasted_iota(jnp.int32, (rows, receivers), 0)
    hot = jnp.where(index == cell_row, 1.0, 0.0).astype(jnp.bfloat16)
    total = lax.dot_general(
        hot, jnp.concatenate(parts, axis=0), (((1,), (1,)), ((), ())), preferred_element_type=jnp.float32
    )
    for t in range(STEPS):
        high, middle, low = (
            total[:, (n * STEPS + t) * depth : (n * STEPS + t + 1) * depth] for n in range(3)
        )
        out[t] = high + (middle + low)
    for copy in others:
        copy.wait()


def depth_matrix(depth):
    row = lax.broadcasted_iota(jnp.int32, (depth, depth), 0)
    col = lax.broadcasted_iota(jnp.int32, (depth, depth), 1)
    apart = jnp.abs(row - col)
    return jnp.where(apart == 1, 16.0, jnp.where(apart == 2, -1.0, 0.0)).astype(jnp.bfloat16)


def depth_neighbours(here, matrix):
    rest = here.reshape(-1, here.shape[-1])
    total = None
    for _ in range(3):
        part = rest.astype(jnp.bfloat16)
        rest = rest - part.astype(jnp.float32)
        term = jnp.dot(part, matrix, preferred_element_type=jnp.float32)
        total = term if total is None else total + term
    return total.reshape(here.shape)


def advance(cur, prev, vel, out, inject, rows, cols, matrix):
    first, count = rows
    col, width = cols
    block = largest_block(count, 28)

    def one(step, carry):
        x = first + step * block
        at = lambda ref, dx, dy: ref[pl.ds(x + dx, block), pl.ds(col + dy, width), :]
        here = at(cur, 0, 0)
        near = at(cur, 1, 0) + at(cur, -1, 0) + at(cur, 0, 1) + at(cur, 0, -1)
        far = at(cur, 2, 0) + at(cur, -2, 0) + at(cur, 0, 2) + at(cur, 0, -2)
        lap = (3.0 * LAP_CENTER) * here + LAP_NEAR * near + LAP_FAR * far
        lap = lap + (1.0 / 12.0) * depth_neighbours(here, matrix)
        new = 2.0 * here - at(prev, 0, 0) + at(vel, 0, 0) * lap
        if inject is not None:
            new = new + inject[pl.ds(x - (PAD - VALID[0]), block), pl.ds(col - PAD // 2, width), :]
        out[pl.ds(x, block), pl.ds(col, width), :] = new
        return carry

    if count == block:
        one(0, 0)
    else:
        lax.fori_loop(0, count // block, one, 0)


def chunk_shift(i, r):
    shots = lax.axis_size("shot")
    held = OFFS // shots
    keeper = lax.rem(lax.axis_index("shot") + r, shots)
    return HALF - (keeper * held + jnp.where(2 * keeper < shots, held - 1 - i, i))


def is_active(aperture):
    tile = lax.axis_index(("gx", "gy"))
    active = aperture[0, 0] == tile
    for k in range(1, aperture.shape[1]):
        active = active | (aperture[0, k] == tile)
    return active


def correlate(lead, lag, strips, keep, strip_rows, outs, slot, i):
    shifts = [chunk_shift(i, r) for r in range(len(outs))]
    place, count = strips

    def one(n, carry):
        for u in range(strip_rows):
            x = HALF + place(n) * strip_rows + u
            for r, out in enumerate(outs):
                total = None
                for t in range(STEPS):
                    term = lead(t, x + shifts[r]) * lag(t, x - shifts[r])
                    total = term if total is None else total + term
                out[n, slot, u] = jnp.where(keep, total, 0.0)
        return carry

    lax.fori_loop(0, count, one, 0)


def inner_rows(t, width_x):
    return PAD + 2 * (t + 1), width_x - 4 * (t + 1)


def outer_rows(t, width_x):
    first, count = inner_rows(t, width_x)
    return (PAD - VALID[t], first + VALID[t] - PAD), (first + count, PAD + width_x + VALID[t] - first - count)


class Sources:
    def __init__(self, src_pos, amps, shape):
        width_x, width_y, depth = shape
        x, y, z, here = locate(src_pos[0], width_x, width_y, depth)
        self.row, self.col, self.here, self.amps = x + PAD, y + PAD, here, amps
        self.lane = lax.broadcasted_iota(jnp.int32, (1, depth), 1)
        self.depth = z

    def add(self, out, t, rows):
        first, count = rows

        @pl.when(self.here & (self.row >= first) & (self.row < first + count))
        def _():
            cells = out[self.row, pl.ds(self.col, 1), :]
            out[self.row, pl.ds(self.col, 1), :] = cells + jnp.where(self.lane == self.depth, self.amps[0, t], 0.0)


def tile_shape(ext):
    return ext.shape[1] - 2 * PAD, ext.shape[2] - 2 * PAD, ext.shape[3]


def column_window(t, width_y):
    return (PAD, width_y) if t == STEPS - 1 else (PAD // 2, width_y + PAD)


def inner_kernel(early, shots, owner, aperture, src_pos, amps, y0, y1, inject, ext_in, *rest):
    count = shots if early else 0
    outs, (ext, s1, s2, s3, sems) = rest[:count], rest[count:]
    width_x, width_y, depth = tile_shape(ext)
    inner_y = pl.ds(PAD, width_y)
    copies = []
    for swap, halo in enumerate((y0, y1)):
        for n, (cols, tile, col) in enumerate(Y_PLACES):
            to = pick(is_upper("gy", swap), PAD + width_y, PAD - cols, cols)
            copies.append(
                pltpu.make_async_copy(
                    halo.at[tile, :, pl.ds(col, cols)], ext.at[n, pl.ds(PAD, width_x), pl.ds(to, cols)],
                    sems.at[len(copies)],
                )
            )
    for copy in copies:
        copy.start()
    keep = is_active(aperture)
    matrix = depth_matrix(depth)
    source = Sources(src_pos, amps, (width_x, width_y, depth))
    for copy in copies:
        copy.wait()
    for f in range(2):
        fields = [ext.at[f], s1.at[f], s2.at[f], s3.at[f]]
        for t in range(STEPS):
            prev = ext.at[2 + f] if t == 0 else fields[t - 1]
            rows = inner_rows(t, width_x)
            advance(
                fields[t], prev, ext.at[4], fields[t + 1], inject.at[t] if f == 1 else None,
                rows, column_window(t, width_y), matrix,
            )
            if f == 0:
                source.add(fields[t + 1], t, rows)
    steps = (s1, s2, s3)
    strip_rows = width_x // owner.shape[0]
    for i in range(early):
        correlate(
            lambda t, x: steps[t][0, x, inner_y, :], lambda t, x: steps[t][1, x, inner_y, :],
            strip_map(0, width_x, strip_rows), keep, strip_rows, outs, i, i,
        )


def outer_kernel(
    early, shots, owner, aperture, src_pos, amps, x0, x1, c0, c1, inject, ext_in, in1, in2, in3, *rest
):
    count = shots if early else 0
    outs, (ext, s1, s2, s3, edge0, edge1, sems, out_sems) = rest[:count], rest[count:]
    width_x, width_y, depth = tile_shape(ext)
    inner_y = pl.ds(PAD, width_y)
    copies = []

    def add(src, dst):
        copies.append(pltpu.make_async_copy(src, dst, sems.at[len(copies)]))

    for swap, corner in enumerate((c0, c1)):
        start = pick(is_upper("gx", swap), PAD + width_x, PAD - CORNER)
        for side in range(2):
            for n, (cols, tile, col) in enumerate(Y_PLACES):
                to = pick(is_upper("gy", side), PAD + width_y, PAD - cols, cols)
                add(corner.at[side, tile, :, pl.ds(col, cols)], ext.at[n, pl.ds(start, CORNER), pl.ds(to, cols)])
    row = 0
    for n in range(5):
        rows = HALF if n < 2 else VALID[0]
        for swap, halo in enumerate((x0, x1)):
            start = pick(is_upper("gx", swap), PAD + width_x, PAD - rows)
            add(halo.at[pl.ds(row, rows)], ext.at[n, pl.ds(start, rows), inner_y])
        row += rows
    for copy in copies:
        copy.start()
    keep = is_active(aperture)
    matrix = depth_matrix(depth)
    source = Sources(src_pos, amps, (width_x, width_y, depth))
    for copy in copies:
        copy.wait()
    chain = [[ext.at[f], s1.at[f], s2.at[f], s3.at[f]] for f in range(2)]
    for t in range(STEPS):
        for f, fields in enumerate(chain):
            prev = ext.at[2 + f] if t == 0 else fields[t - 1]
            for rows in outer_rows(t, width_x):
                advance(
                    fields[t], prev, ext.at[4], fields[t + 1], inject.at[t] if f == 1 else None,
                    rows, column_window(t, width_y), matrix,
                )
        for rows in outer_rows(t, width_x):
            source.add(chain[0][t + 1], t, rows)
    steps = (s1, s2, s3)
    sends = []
    row = 0
    for t in range(STEPS):
        rows = HALF - VALID[t]
        for f in range(2):
            for swap, edge in enumerate((edge0, edge1)):
                start = pick(is_upper("gx", swap), PAD + width_x - HALF, PAD + VALID[t])
                sends.append(
                    pltpu.make_async_copy(
                        steps[t].at[f, pl.ds(start, rows), inner_y], edge.at[pl.ds(row, rows)],
                        out_sems.at[len(sends)],
                    )
                )
                sends[-1].start()
            row += rows
    strip_rows = width_x // owner.shape[0]
    for i in range(early):
        correlate(
            lambda t, x: steps[t][0, x, inner_y, :], lambda t, x: steps[t][1, x, inner_y, :],
            strip_map(1, width_x, strip_rows), keep, strip_rows, outs, i, i,
        )
    for copy in sends:
        copy.wait()


def strip_map(part, width_x, strip_rows):
    side = HALF // strip_rows
    middle = (width_x - 2 * HALF) // strip_rows
    if part == 0:
        return lambda n: n + side, middle
    return lambda n: n + jnp.where(n < side, 0, middle), 2 * side


def rest_kernel(part, groups, shots, owner, aperture, *rest):
    count = len(groups) * shots
    if part == 0:
        (s1, s2, s3), rest = rest[:3], rest[3:]
        results, last, rest = rest[:count], rest[count : count + 2], rest[count + 2 :]
    else:
        edges, rest = rest[:2], rest[6:]
        results, (s1, s2, s3), last, rest = rest[:count], rest[count : count + 3], (), rest[count + 3 :]
    outs, (sems, out_sems) = (results[0], *rest[: count - 1]), rest[count - 1 :]
    steps = (s1, s2, s3)
    width_x, width_y, _ = tile_shape(s1)
    inner_y = pl.ds(PAD, width_y)
    copies = []
    row = 0
    for t in range(STEPS):
        rows = HALF - VALID[t]
        for f in range(2 * part):
            for swap, edge in enumerate(edges):
                start = pick(is_upper("gx", swap), PAD + width_x + VALID[t], 0)
                copies.append(
                    pltpu.make_async_copy(
                        edge.at[pl.ds(row, rows)], steps[t].at[f, pl.ds(start, rows), inner_y],
                        sems.at[len(copies)],
                    )
                )
            row += rows
    keep = is_active(aperture)
    run_copies(copies)
    sends = []

    def send(src, dst):
        sends.append(pltpu.make_async_copy(src, dst, out_sems.at[len(sends)]))
        sends[-1].start()

    strip_rows = width_x // owner.shape[0]
    for g, group in enumerate(groups):
        for slot, i in enumerate(group):
            places = slice(g * shots, (g + 1) * shots)
            correlate(
                lambda t, x: steps[t][0, x, inner_y, :], lambda t, x: steps[t][1, x, inner_y, :],
                strip_map(part, width_x, strip_rows), keep, strip_rows, outs[places], slot, i,
            )
            for out, result in zip(outs[places], results[places]):
                if out is not result:
                    send(out.at[:, slot], result.at[:, slot])
    for f, out in enumerate(last):
        send(s3.at[f, pl.ds(PAD, width_x), inner_y], out.at[0])
    for copy in sends:
        copy.wait()


def sum_kernel(part, shots, owner, *refs):
    parts = refs[:shots]
    total, cells, sems = refs[shots + part :]
    tiles = owner.shape[0]
    tile = lax.axis_index(("gx", "gy"))
    strip, count = strip_map(part, parts[0].shape[2] * tiles, parts[0].shape[2])
    copies = []
    for n in range(count):
        one = parts[0][n]
        for other in parts[1:]:
            one = one + other[n]
        cells[n] = one
        copies.append(pltpu.make_async_copy(cells.at[n], total.at[owner[tile, strip(n)]], sems.at[n]))
        copies[-1].start()
    for copy in copies:
        copy.wait()


def place_kernel(group, held, old, piece, out, sems):
    shots = lax.axis_size("shot")
    copies = []
    for slot, i in enumerate(group):
        where = jnp.where(2 * lax.axis_index("shot") < shots, held - 1 - i, i)
        copies.append(pltpu.make_async_copy(piece.at[:, slot], out.at[0, where], sems.at[slot]))
    run_copies(copies)


PACK_LIMIT = 63_400_000
SPREAD_LIMIT = 48 * 1024 * 1024


def body(
    vel_coef, src_prev, src_cur, rcv_prev, rcv_cur, src_pos, src_amp, rcv_pos, rcv_data, aperture, owner
):
    f32 = jnp.float32
    width_x, width_y, depth = vel_coef.shape
    n_gx, n_gy, shots = lax.axis_size("gx"), lax.axis_size("gy"), lax.axis_size("shot")
    tiles = n_gx * n_gy
    strip_rows = width_x // tiles
    shot = lax.axis_index("shot")
    swaps_x, swaps_y = swap_pairs(n_gx), swap_pairs(n_gy)

    held = OFFS // shots
    chunk_offset = [
        [o * held + (held - 1 - i if 2 * o < shots else i) for o in range(shots)] for i in range(held)
    ]
    early = 0
    while early < held and all(abs(HALF - h) <= VALID[-1] for h in chunk_offset[early]):
        early += 1
    ext_x, ext_y = width_x + 2 * VALID[0], width_y + PAD

    small = pltpu.CompilerParams(vmem_limit_bytes=16 * 1024 * 1024)
    big = pltpu.CompilerParams(vmem_limit_bytes=24 * 1024 * 1024)
    x_rows = 2 * HALF + 3 * VALID[0]
    args = (vel_coef, src_prev, src_cur, rcv_prev, rcv_cur)

    x_part = jax.ShapeDtypeStruct((x_rows, width_y, depth), f32)
    y_part = jax.ShapeDtypeStruct((Y_TILES, width_x, PAD, depth), f32)
    receivers = rcv_pos.shape[1]
    *sends, positions, values = pl.pallas_call(
        pack_kernel,
        out_shape=(x_part, x_part, y_part, y_part)
        + (pltpu.VMEM((1, receivers), jnp.int32), pltpu.VMEM((1, STEPS * receivers), f32)),
        in_specs=[ANY] * 7,
        out_specs=(ANY,) * 4 + (VMEM,) * 2,
        scratch_shapes=[pltpu.VMEM(part.shape, f32) for part in (x_part, x_part, y_part, y_part)]
        + [pltpu.SemaphoreType.DMA((22,)), pltpu.SemaphoreType.DMA((4,))],
        compiler_params=pltpu.CompilerParams(vmem_limit_bytes=PACK_LIMIT),
        name="pack_halos",
    )(rcv_pos, rcv_data.reshape(1, STEPS * receivers), *args)
    halos = [lax.ppermute(sends[n], "gx", swaps_x[n]) for n in range(2)]
    halos += [lax.ppermute(sends[2 + n], "gy", swaps_y[n]) for n in range(2)]

    span = (width_x + 2 * PAD, width_y + 2 * PAD, depth)
    padded = pltpu.VMEM((5,) + span, f32)
    step = pltpu.VMEM((2,) + span, f32)
    inject, ext = pl.pallas_call(
        spread_kernel,
        out_shape=(pltpu.VMEM((STEPS, ext_x * ext_y, depth), f32), padded),
        in_specs=[VMEM] * 2 + [ANY] * 5,
        out_specs=(VMEM, VMEM),
        scratch_shapes=[pltpu.SemaphoreType.DMA((5,))],
        compiler_params=pltpu.CompilerParams(vmem_limit_bytes=SPREAD_LIMIT),
        cost_estimate=pl.CostEstimate(
            flops=6 * ext_x * ext_y * receivers * depth * STEPS, bytes_accessed=4 * STEPS * ext_x * ext_y * depth,
            transcendentals=0),
        name="spread_receivers",
    )(positions, values, *args)
    spread = inject.reshape(STEPS, ext_x, ext_y, depth)

    corner = jax.ShapeDtypeStruct((2, Y_TILES, CORNER, PAD, depth), f32)
    corners = pl.pallas_call(
        corner_kernel,
        out_shape=(corner, corner),
        in_specs=[ANY] * 3,
        out_specs=(VMEM, VMEM),
        scratch_shapes=[pltpu.SemaphoreType.DMA((4,))],
        compiler_params=big,
        name="pack_corners",
    )(halos[2], halos[3], inject)
    halos += [lax.ppermute(corners[n], "gx", swaps_x[n]) for n in range(2)]

    def piece(strips, group):
        return jax.ShapeDtypeStruct((strips, len(group), strip_rows, width_y, depth), f32)

    first = tuple(range(early))
    groups = [tuple(range(i, min(i + 3, held))) for i in range(early, held, 3)]
    edge_rows = 2 * sum(HALF - v for v in VALID)
    edge = jax.ShapeDtypeStruct((edge_rows, width_y, depth), f32)
    step_ops = 30 * width_x * width_y * depth * STEPS
    tables = (owner, aperture)
    middle = (width_x - 2 * HALF) // strip_rows
    count = shots if early else 0
    inner = pl.pallas_call(
        functools.partial(inner_kernel, early, shots),
        out_shape=(piece(middle, first),) * count + (padded,) + (step,) * 3,
        in_specs=[SMEM] * 4 + [ANY] * 2 + [VMEM] * 2,
        out_specs=(VMEM,) * (count + 4),
        scratch_shapes=[pltpu.SemaphoreType.DMA((10,))],
        input_output_aliases={7: count},
        compiler_params=big,
        cost_estimate=pl.CostEstimate(flops=step_ops, bytes_accessed=12 * 2**20, transcendentals=0),
        name="inner_steps",
    )(*tables, src_pos, src_amp, *halos[2:4], spread, ext)
    inner_pieces, inner = inner[:count], inner[count:]
    outer = pl.pallas_call(
        functools.partial(outer_kernel, early, shots),
        out_shape=(piece(tiles - middle, first),) * count + (padded,) + (step,) * 3 + (edge, edge),
        in_specs=[SMEM] * 4 + [ANY] * 4 + [VMEM] * 5,
        out_specs=(VMEM,) * (count + 6),
        scratch_shapes=[pltpu.SemaphoreType.DMA((30,)), pltpu.SemaphoreType.DMA((12,))],
        input_output_aliases={9 + n: count + n for n in range(4)},
        compiler_params=big,
        cost_estimate=pl.CostEstimate(flops=step_ops, bytes_accessed=12 * 2**20, transcendentals=0),
        name="outer_steps",
    )(*tables, src_pos, src_amp, *halos[:2], *halos[4:], spread, *inner)
    outer_pieces, outer, edges = outer[:count], outer[count + 1 : count + 4], outer[count + 4 :]
    edges = [lax.ppermute(edges[n], "gx", swaps_x[n]) for n in range(2)]
    field = jax.ShapeDtypeStruct(src_cur.shape, f32)

    def others(part, *operands):
        strips = middle if part == 0 else tiles - middle
        shapes = [piece(strips, g).shape for g in groups for _ in range(shots)]
        extra = (field, field) if part == 0 else (step,) * 3
        result = pl.pallas_call(
            functools.partial(rest_kernel, part, groups, shots),
            out_shape=(jax.ShapeDtypeStruct(shapes[0], f32),)
            + tuple(pltpu.HBM(shape, f32) for shape in shapes[1:])
            + extra,
            in_specs=[SMEM] * 2 + ([VMEM] * 3 if part == 0 else [ANY] * 2 + [VMEM] * 3 + [ANY]),
            out_specs=(VMEM,) + (ANY,) * (len(shapes) - 1) + ((ANY,) * 2 if part == 0 else (VMEM,) * 3),
            scratch_shapes=[pltpu.VMEM(shape, f32) for shape in shapes[1:]]
            + [pltpu.SemaphoreType.DMA((12,)), pltpu.SemaphoreType.DMA((2 + held * shots,))],
            input_output_aliases={4 + n: len(shapes) + n for n in range(3 * part)},
            compiler_params=big,
            cost_estimate=pl.CostEstimate(
                flops=5 * OFFS * width_x * width_y * depth, bytes_accessed=12 * 2**20, transcendentals=0),
            name=("far_strips", "near_strips")[part],
        )(*tables, *operands)
        return result[: len(shapes)], result[len(shapes) :]

    def swapped(cells):
        return [
            lax.ppermute(one, "shot", [(s, (s + r + 1) % shots) for s in range(shots)])
            for r, one in enumerate(cells)
        ]

    long_cost = pl.CostEstimate(flops=2**37, bytes_accessed=2**28, transcendentals=0)

    def summed(kept, coming, group):
        total = []
        for part in range(2):
            cells = list(kept[part]) + list(coming[part])
            total = [
                pl.pallas_call(
                    functools.partial(sum_kernel, part, shots),
                    out_shape=piece(tiles, group),
                    in_specs=[SMEM] + [VMEM] * shots + [ANY] * part,
                    out_specs=ANY,
                    scratch_shapes=[
                        pltpu.VMEM(cells[0].shape, f32), pltpu.SemaphoreType.DMA((cells[0].shape[0],))],
                    input_output_aliases={1 + shots: 0} if part else {},
                    compiler_params=small,
                    cost_estimate=pl.CostEstimate(flops=(2**20, 2**34)[part], bytes_accessed=2**20, transcendentals=0),
                    name=("sum_far", "sum_near")[part],
                )(owner, *cells, *total)
            ]
        return total[0]

    totals = []
    coming = []
    if early:
        both = (inner_pieces, outer_pieces)
        coming = [swapped(cells[1:]) for cells in both]
        totals.append(summed([cells[:1] for cells in both], coming, first))
    far, (src_next, rcv_next) = others(0, *outer)
    near, _ = others(1, *edges, *outer, totals[0] if early else edges[0])
    for g, group in enumerate(groups):
        both = [cells[g * shots : (g + 1) * shots] for cells in (far, near)]
        going = [cells[1:] for cells in both]
        if coming:
            if g == 0 and early:
                (going[0], coming) = lax.optimization_barrier((going[0], coming))
            else:
                (going, coming) = lax.optimization_barrier((going, coming))
        coming = [swapped(cells) for cells in going]
        totals.append(summed([cells[:1] for cells in both], coming, group))
    gathers = jnp.zeros((1, held, tiles, strip_rows, width_y, depth), f32)
    chunks = ([first] if early else []) + groups
    for n, (group, total) in enumerate(zip(chunks, totals)):
        arrived = lax.all_to_all(total, ("gx", "gy"), split_axis=0, concat_axis=0, tiled=True)
        if n < len(chunks) - 1:
            for slot, i in enumerate(group):
                where = jnp.where(2 * shot < shots, held - 1 - i, i)
                gathers = lax.dynamic_update_slice(gathers, arrived[None, None, :, slot], (0, where, 0, 0, 0, 0))
            continue
        gathers = pl.pallas_call(
            functools.partial(place_kernel, group, held),
            out_shape=jax.ShapeDtypeStruct(gathers.shape, f32),
            in_specs=[ANY, VMEM],
            out_specs=ANY,
            scratch_shapes=[pltpu.SemaphoreType.DMA((len(group),))],
            input_output_aliases={0: 0},
            compiler_params=small,
            name="place_strips",
        )(gathers, arrived)
    return src_next, rcv_next, gathers


def solution(mesh):
    return jax.shard_map(
        body,
        mesh=mesh,
        in_specs=(
            P("gx", "gy", None),
            P("shot", "gx", "gy", None),
            P("shot", "gx", "gy", None),
            P("shot", "gx", "gy", None),
            P("shot", "gx", "gy", None),
            P("shot"),
            P("shot", None),
            P("shot", None),
            P("shot", None, None),
            P("shot", None),
            P(),
        ),
        out_specs=(
            P("shot", "gx", "gy", None),
            P("shot", "gx", "gy", None),
            P(("gx", "gy"), "shot", None, None, None, None),
        ),
        check_vma=False,
    )
```

```python
import functools

import jax
import jax.numpy as jnp
from jax import lax
from jax.experimental import pallas as pl
from jax.experimental.pallas import tpu as pltpu
from jax.sharding import PartitionSpec as P

OFFS = 16
STEPS = 3
HALF = 8
PAD = 8
VALID = (6, 4, 2)
CORNER = 6

LAP_CENTER = -2.5
LAP_NEAR = 4.0 / 3.0
LAP_FAR = -1.0 / 12.0

ANY = pl.BlockSpec(memory_space=pl.ANY)
SMEM = pl.BlockSpec(memory_space=pltpu.SMEM)
VMEM = pl.BlockSpec(memory_space=pltpu.VMEM)


def swap_pairs(count):
    first = [(i, i ^ 1) for i in range(count) if (i ^ 1) < count]
    second = []
    for i in range(1, count - 1, 2):
        second += [(i, i + 1), (i + 1, i)]
    return first, second


def largest_block(count, limit):
    return max(n for n in range(1, limit + 1) if count % n == 0)


def run_copies(copies):
    for copy in copies:
        copy.start()
    for copy in copies:
        copy.wait()


def is_upper(axis, swap):
    return lax.rem(lax.axis_index(axis) + swap, 2) == 0


def pick(condition, upper, lower, multiple=1):
    return pl.multiple_of(jnp.where(condition, upper, lower), multiple)


Y_PLACES = ((PAD, 0, 0), (PAD, 1, 0), (PAD // 2, 2, 0), (PAD // 2, 2, PAD // 2), (PAD, 3, 0))
Y_TILES = 4


def pack_kernel(
    positions_from, values_from, vel, src_prev, src_cur, rcv_prev, rcv_cur, x0, x1, y0, y1, positions, values, *scratch
):
    *buffers, sems, out_sems = scratch
    small = [
        pltpu.make_async_copy(positions_from, positions, sems.at[20]),
        pltpu.make_async_copy(values_from, values, sems.at[21]),
    ]
    width_x, width_y, depth = vel.shape
    fields = (src_cur.at[0], rcv_cur.at[0], src_prev.at[0], rcv_prev.at[0], vel)
    jobs = []
    count = 0
    for swap in range(2):
        copies = []
        for n, field in enumerate(fields):
            cols, tile, col = Y_PLACES[n]
            start = pick(is_upper("gy", swap), width_y - cols, 0, cols)
            copies.append(
                pltpu.make_async_copy(
                    field.at[:, pl.ds(start, cols)], buffers[2 + swap].at[tile, :, pl.ds(col, cols)],
                    sems.at[count],
                )
            )
            count += 1
        jobs.append((copies, buffers[2 + swap], (y0, y1)[swap]))
    for swap in range(2):
        row = 0
        copies = []
        for n, field in enumerate(fields):
            rows = HALF if n < 2 else VALID[0]
            start = pick(is_upper("gx", swap), width_x - rows, 0)
            copies.append(
                pltpu.make_async_copy(
                    field.at[pl.ds(start, rows)], buffers[swap].at[pl.ds(row, rows)], sems.at[count])
            )
            row += rows
            count += 1
        jobs.append((copies, buffers[swap], (x0, x1)[swap]))
    for copies in [copies for copies, _, _ in jobs] + [small]:
        for copy in copies:
            copy.start()
    sends = []
    for n, (copies, buffer, out) in enumerate(jobs):
        for copy in copies:
            copy.wait()
        sends.append(pltpu.make_async_copy(buffer, out, out_sems.at[n]))
        sends[-1].start()
    for copy in small + sends:
        copy.wait()


def corner_kernel(y0, y1, late, c0, c1, sems):
    width_x = y0.shape[1]
    copies = []
    for swap, out in enumerate((c0, c1)):
        start = pick(is_upper("gx", swap), width_x - CORNER, 0)
        for n, halo in enumerate((y0, y1)):
            copies.append(
                pltpu.make_async_copy(halo.at[:, pl.ds(start, CORNER)], out.at[n], sems.at[len(copies)])
            )
    run_copies(copies)


def locate(position, width_x, width_y, depth):
    grid_y = width_y * lax.axis_size("gy")
    x = lax.div(position, grid_y * depth) - lax.axis_index("gx") * width_x
    y = lax.rem(lax.div(position, depth), grid_y) - lax.axis_index("gy") * width_y
    reach = VALID[0]
    inside = (x >= -reach) & (x < width_x + reach) & (y >= -PAD // 2) & (y < width_y + PAD // 2)
    return x, y, lax.rem(position, depth), inside


def spread_kernel(positions, values, vel, src_prev, src_cur, rcv_prev, rcv_cur, out, ext, sems):
    width_x, width_y, _ = vel.shape
    fields = (src_cur.at[0], rcv_cur.at[0], src_prev.at[0], rcv_prev.at[0], vel)
    others = [
        pltpu.make_async_copy(field, ext.at[n, pl.ds(PAD, width_x), pl.ds(PAD, width_y)], sems.at[n])
        for n, field in enumerate(fields)
    ]
    for copy in others:
        copy.start()
    rows, depth = out.shape[1], out.shape[2]
    receivers = positions.shape[1]
    x, y, depths, inside = locate(positions[...], width_x, width_y, depth)
    cell_row = jnp.where(inside, (x + VALID[0]) * (width_y + PAD) + y + PAD // 2, -1)
    lanes = lax.broadcasted_iota(jnp.int32, (depth, receivers), 0)
    rest = jnp.concatenate(
        [
            jnp.where(lanes == depths, values[:, t * receivers : (t + 1) * receivers], 0.0)
            for t in range(STEPS)
        ],
        axis=0,
    )
    parts = []
    for _ in range(3):
        parts.append(rest.astype(jnp.bfloat16))
        rest = rest - parts[-1].astype(jnp.float32)
    index = lax.broadcasted_iota(jnp.int32, (rows, receivers), 0)
    hot = jnp.where(index == cell_row, 1.0, 0.0).astype(jnp.bfloat16)
    total = lax.dot_general(
        hot, jnp.concatenate(parts, axis=0), (((1,), (1,)), ((), ())), preferred_element_type=jnp.float32
    )
    for t in range(STEPS):
        high, middle, low = (
            total[:, (n * STEPS + t) * depth : (n * STEPS + t + 1) * depth] for n in range(3)
        )
        out[t] = high + (middle + low)
    for copy in others:
        copy.wait()


def depth_matrix(depth):
    row = lax.broadcasted_iota(jnp.int32, (depth, depth), 0)
    col = lax.broadcasted_iota(jnp.int32, (depth, depth), 1)
    apart = jnp.abs(row - col)
    return jnp.where(apart == 1, 16.0, jnp.where(apart == 2, -1.0, 0.0)).astype(jnp.bfloat16)


def depth_neighbours(here, matrix):
    rest = here.reshape(-1, here.shape[-1])
    total = None
    for _ in range(3):
        part = rest.astype(jnp.bfloat16)
        rest = rest - part.astype(jnp.float32)
        term = jnp.dot(part, matrix, preferred_element_type=jnp.float32)
        total = term if total is None else total + term
    return total.reshape(here.shape)


def advance(cur, prev, vel, out, inject, rows, cols, matrix):
    first, count = rows
    col, width = cols
    block = largest_block(count, 28)

    def one(step, carry):
        x = first + step * block
        at = lambda ref, dx, dy: ref[pl.ds(x + dx, block), pl.ds(col + dy, width), :]
        here = at(cur, 0, 0)
        near = at(cur, 1, 0) + at(cur, -1, 0) + at(cur, 0, 1) + at(cur, 0, -1)
        far = at(cur, 2, 0) + at(cur, -2, 0) + at(cur, 0, 2) + at(cur, 0, -2)
        lap = (3.0 * LAP_CENTER) * here + LAP_NEAR * near + LAP_FAR * far
        lap = lap + (1.0 / 12.0) * depth_neighbours(here, matrix)
        new = 2.0 * here - at(prev, 0, 0) + at(vel, 0, 0) * lap
        if inject is not None:
            new = new + inject[pl.ds(x - (PAD - VALID[0]), block), pl.ds(col - PAD // 2, width), :]
        out[pl.ds(x, block), pl.ds(col, width), :] = new
        return carry

    if count == block:
        one(0, 0)
    else:
        lax.fori_loop(0, count // block, one, 0)


def chunk_shift(i, r):
    shots = lax.axis_size("shot")
    held = OFFS // shots
    keeper = lax.rem(lax.axis_index("shot") + r, shots)
    return HALF - (keeper * held + jnp.where(2 * keeper < shots, held - 1 - i, i))


def is_active(aperture):
    tile = lax.axis_index(("gx", "gy"))
    active = aperture[0, 0] == tile
    for k in range(1, aperture.shape[1]):
        active = active | (aperture[0, k] == tile)
    return active


def correlate(lead, lag, strips, keep, strip_rows, outs, slot, i):
    shifts = [chunk_shift(i, r) for r in range(len(outs))]
    place, count = strips

    def one(n, carry):
        for u in range(strip_rows):
            x = HALF + place(n) * strip_rows + u
            for r, out in enumerate(outs):
                total = None
                for t in range(STEPS):
                    term = lead(t, x + shifts[r]) * lag(t, x - shifts[r])
                    total = term if total is None else total + term
                out[n, slot, u] = jnp.where(keep, total, 0.0)
        return carry

    lax.fori_loop(0, count, one, 0)


def inner_rows(t, width_x):
    return PAD + 2 * (t + 1), width_x - 4 * (t + 1)


def outer_rows(t, width_x):
    first, count = inner_rows(t, width_x)
    return (PAD - VALID[t], first + VALID[t] - PAD), (first + count, PAD + width_x + VALID[t] - first - count)


class Sources:
    def __init__(self, src_pos, amps, shape):
        width_x, width_y, depth = shape
        x, y, z, here = locate(src_pos[0], width_x, width_y, depth)
        self.row, self.col, self.here, self.amps = x + PAD, y + PAD, here, amps
        self.lane = lax.broadcasted_iota(jnp.int32, (1, depth), 1)
        self.depth = z

    def add(self, out, t, rows):
        first, count = rows

        @pl.when(self.here & (self.row >= first) & (self.row < first + count))
        def _():
            cells = out[self.row, pl.ds(self.col, 1), :]
            out[self.row, pl.ds(self.col, 1), :] = cells + jnp.where(self.lane == self.depth, self.amps[0, t], 0.0)


def tile_shape(ext):
    return ext.shape[1] - 2 * PAD, ext.shape[2] - 2 * PAD, ext.shape[3]


def column_window(t, width_y):
    return (PAD, width_y) if t == STEPS - 1 else (PAD // 2, width_y + PAD)


def inner_kernel(early, shots, owner, aperture, src_pos, amps, y0, y1, inject, ext_in, *rest):
    count = shots if early else 0
    outs, (ext, s1, s2, s3, sems) = rest[:count], rest[count:]
    width_x, width_y, depth = tile_shape(ext)
    inner_y = pl.ds(PAD, width_y)
    copies = []
    for swap, halo in enumerate((y0, y1)):
        for n, (cols, tile, col) in enumerate(Y_PLACES):
            to = pick(is_upper("gy", swap), PAD + width_y, PAD - cols, cols)
            copies.append(
                pltpu.make_async_copy(
                    halo.at[tile, :, pl.ds(col, cols)], ext.at[n, pl.ds(PAD, width_x), pl.ds(to, cols)],
                    sems.at[len(copies)],
                )
            )
    for copy in copies:
        copy.start()
    keep = is_active(aperture)
    matrix = depth_matrix(depth)
    source = Sources(src_pos, amps, (width_x, width_y, depth))
    for copy in copies:
        copy.wait()
    for f in range(2):
        fields = [ext.at[f], s1.at[f], s2.at[f], s3.at[f]]
        for t in range(STEPS):
            prev = ext.at[2 + f] if t == 0 else fields[t - 1]
            rows = inner_rows(t, width_x)
            advance(
                fields[t], prev, ext.at[4], fields[t + 1], inject.at[t] if f == 1 else None,
                rows, column_window(t, width_y), matrix,
            )
            if f == 0:
                source.add(fields[t + 1], t, rows)
    steps = (s1, s2, s3)
    strip_rows = width_x // owner.shape[0]
    for i in range(early):
        correlate(
            lambda t, x: steps[t][0, x, inner_y, :], lambda t, x: steps[t][1, x, inner_y, :],
            strip_map(0, width_x, strip_rows), keep, strip_rows, outs, i, i,
        )


def outer_kernel(
    early, shots, owner, aperture, src_pos, amps, x0, x1, c0, c1, inject, ext_in, in1, in2, in3, *rest
):
    count = shots if early else 0
    outs, (ext, s1, s2, s3, edge0, edge1, sems, out_sems) = rest[:count], rest[count:]
    width_x, width_y, depth = tile_shape(ext)
    inner_y = pl.ds(PAD, width_y)
    copies = []

    def add(src, dst):
        copies.append(pltpu.make_async_copy(src, dst, sems.at[len(copies)]))

    for swap, corner in enumerate((c0, c1)):
        start = pick(is_upper("gx", swap), PAD + width_x, PAD - CORNER)
        for side in range(2):
            for n, (cols, tile, col) in enumerate(Y_PLACES):
                to = pick(is_upper("gy", side), PAD + width_y, PAD - cols, cols)
                add(corner.at[side, tile, :, pl.ds(col, cols)], ext.at[n, pl.ds(start, CORNER), pl.ds(to, cols)])
    row = 0
    for n in range(5):
        rows = HALF if n < 2 else VALID[0]
        for swap, halo in enumerate((x0, x1)):
            start = pick(is_upper("gx", swap), PAD + width_x, PAD - rows)
            add(halo.at[pl.ds(row, rows)], ext.at[n, pl.ds(start, rows), inner_y])
        row += rows
    for copy in copies:
        copy.start()
    keep = is_active(aperture)
    matrix = depth_matrix(depth)
    source = Sources(src_pos, amps, (width_x, width_y, depth))
    for copy in copies:
        copy.wait()
    chain = [[ext.at[f], s1.at[f], s2.at[f], s3.at[f]] for f in range(2)]
    for t in range(STEPS):
        for f, fields in enumerate(chain):
            prev = ext.at[2 + f] if t == 0 else fields[t - 1]
            for rows in outer_rows(t, width_x):
                advance(
                    fields[t], prev, ext.at[4], fields[t + 1], inject.at[t] if f == 1 else None,
                    rows, column_window(t, width_y), matrix,
                )
        for rows in outer_rows(t, width_x):
            source.add(chain[0][t + 1], t, rows)
    steps = (s1, s2, s3)
    sends = []
    row = 0
    for t in range(STEPS):
        rows = HALF - VALID[t]
        for f in range(2):
            for swap, edge in enumerate((edge0, edge1)):
                start = pick(is_upper("gx", swap), PAD + width_x - HALF, PAD + VALID[t])
                sends.append(
                    pltpu.make_async_copy(
                        steps[t].at[f, pl.ds(start, rows), inner_y], edge.at[pl.ds(row, rows)],
                        out_sems.at[len(sends)],
                    )
                )
                sends[-1].start()
            row += rows
    strip_rows = width_x // owner.shape[0]
    for i in range(early):
        correlate(
            lambda t, x: steps[t][0, x, inner_y, :], lambda t, x: steps[t][1, x, inner_y, :],
            strip_map(1, width_x, strip_rows), keep, strip_rows, outs, i, i,
        )
    for copy in sends:
        copy.wait()


def strip_map(part, width_x, strip_rows):
    side = HALF // strip_rows
    middle = (width_x - 2 * HALF) // strip_rows
    if part == 0:
        return lambda n: n + side, middle
    return lambda n: n + jnp.where(n < side, 0, middle), 2 * side


def rest_kernel(part, groups, shots, owner, aperture, *rest):
    count = len(groups) * shots
    if part == 0:
        (s1, s2, s3), rest = rest[:3], rest[3:]
        results, last, rest = rest[:count], rest[count : count + 2], rest[count + 2 :]
    else:
        edges, rest = rest[:2], rest[6:]
        results, (s1, s2, s3), last, rest = rest[:count], rest[count : count + 3], (), rest[count + 3 :]
    outs, (sems, out_sems) = (results[0], *rest[: count - 1]), rest[count - 1 :]
    steps = (s1, s2, s3)
    width_x, width_y, _ = tile_shape(s1)
    inner_y = pl.ds(PAD, width_y)
    copies = []
    row = 0
    for t in range(STEPS):
        rows = HALF - VALID[t]
        for f in range(2 * part):
            for swap, edge in enumerate(edges):
                start = pick(is_upper("gx", swap), PAD + width_x + VALID[t], 0)
                copies.append(
                    pltpu.make_async_copy(
                        edge.at[pl.ds(row, rows)], steps[t].at[f, pl.ds(start, rows), inner_y],
                        sems.at[len(copies)],
                    )
                )
            row += rows
    keep = is_active(aperture)
    run_copies(copies)
    sends = []

    def send(src, dst):
        sends.append(pltpu.make_async_copy(src, dst, out_sems.at[len(sends)]))
        sends[-1].start()

    strip_rows = width_x // owner.shape[0]
    for g, group in enumerate(groups):
        for slot, i in enumerate(group):
            places = slice(g * shots, (g + 1) * shots)
            correlate(
                lambda t, x: steps[t][0, x, inner_y, :], lambda t, x: steps[t][1, x, inner_y, :],
                strip_map(part, width_x, strip_rows), keep, strip_rows, outs[places], slot, i,
            )
            for out, result in zip(outs[places], results[places]):
                if out is not result:
                    send(out.at[:, slot], result.at[:, slot])
    for f, out in enumerate(last):
        send(s3.at[f, pl.ds(PAD, width_x), inner_y], out.at[0])
    for copy in sends:
        copy.wait()


def sum_kernel(part, shots, owner, *refs):
    parts = refs[:shots]
    total, cells, sems = refs[shots + part :]
    tiles = owner.shape[0]
    tile = lax.axis_index(("gx", "gy"))
    strip, count = strip_map(part, parts[0].shape[2] * tiles, parts[0].shape[2])
    copies = []
    for n in range(count):
        one = parts[0][n]
        for other in parts[1:]:
            one = one + other[n]
        cells[n] = one
        copies.append(pltpu.make_async_copy(cells.at[n], total.at[owner[tile, strip(n)]], sems.at[n]))
        copies[-1].start()
    for copy in copies:
        copy.wait()


def place_kernel(group, held, old, piece, out, sems):
    shots = lax.axis_size("shot")
    copies = []
    for slot, i in enumerate(group):
        where = jnp.where(2 * lax.axis_index("shot") < shots, held - 1 - i, i)
        copies.append(pltpu.make_async_copy(piece.at[:, slot], out.at[0, where], sems.at[slot]))
    run_copies(copies)


PACK_LIMIT = 63_400_000
SPREAD_LIMIT = 48 * 1024 * 1024


SUM_COSTS = ((2**20, 2**34), (2**20, 2**35), (3 * 2**33, 2**20))


def body(
    vel_coef, src_prev, src_cur, rcv_prev, rcv_cur, src_pos, src_amp, rcv_pos, rcv_data, aperture, owner
):
    f32 = jnp.float32
    width_x, width_y, depth = vel_coef.shape
    n_gx, n_gy, shots = lax.axis_size("gx"), lax.axis_size("gy"), lax.axis_size("shot")
    tiles = n_gx * n_gy
    strip_rows = width_x // tiles
    shot = lax.axis_index("shot")
    swaps_x, swaps_y = swap_pairs(n_gx), swap_pairs(n_gy)

    held = OFFS // shots
    chunk_offset = [
        [o * held + (held - 1 - i if 2 * o < shots else i) for o in range(shots)] for i in range(held)
    ]
    early = 0
    while early < held and all(abs(HALF - h) <= VALID[-1] for h in chunk_offset[early]):
        early += 1
    ext_x, ext_y = width_x + 2 * VALID[0], width_y + PAD

    small = pltpu.CompilerParams(vmem_limit_bytes=16 * 1024 * 1024)
    big = pltpu.CompilerParams(vmem_limit_bytes=24 * 1024 * 1024)
    x_rows = 2 * HALF + 3 * VALID[0]
    args = (vel_coef, src_prev, src_cur, rcv_prev, rcv_cur)

    x_part = jax.ShapeDtypeStruct((x_rows, width_y, depth), f32)
    y_part = jax.ShapeDtypeStruct((Y_TILES, width_x, PAD, depth), f32)
    receivers = rcv_pos.shape[1]
    *sends, positions, values = pl.pallas_call(
        pack_kernel,
        out_shape=(x_part, x_part, y_part, y_part)
        + (pltpu.VMEM((1, receivers), jnp.int32), pltpu.VMEM((1, STEPS * receivers), f32)),
        in_specs=[ANY] * 7,
        out_specs=(ANY,) * 4 + (VMEM,) * 2,
        scratch_shapes=[pltpu.VMEM(part.shape, f32) for part in (x_part, x_part, y_part, y_part)]
        + [pltpu.SemaphoreType.DMA((22,)), pltpu.SemaphoreType.DMA((4,))],
        compiler_params=pltpu.CompilerParams(vmem_limit_bytes=PACK_LIMIT),
        name="pack_halos",
    )(rcv_pos, rcv_data.reshape(1, STEPS * receivers), *args)
    halos = [lax.ppermute(sends[n], "gx", swaps_x[n]) for n in range(2)]
    halos += [lax.ppermute(sends[2 + n], "gy", swaps_y[n]) for n in range(2)]

    span = (width_x + 2 * PAD, width_y + 2 * PAD, depth)
    padded = pltpu.VMEM((5,) + span, f32)
    step = pltpu.VMEM((2,) + span, f32)
    inject, ext = pl.pallas_call(
        spread_kernel,
        out_shape=(pltpu.VMEM((STEPS, ext_x * ext_y, depth), f32), padded),
        in_specs=[VMEM] * 2 + [ANY] * 5,
        out_specs=(VMEM, VMEM),
        scratch_shapes=[pltpu.SemaphoreType.DMA((5,))],
        compiler_params=pltpu.CompilerParams(vmem_limit_bytes=SPREAD_LIMIT),
        cost_estimate=pl.CostEstimate(
            flops=6 * ext_x * ext_y * receivers * depth * STEPS, bytes_accessed=4 * STEPS * ext_x * ext_y * depth,
            transcendentals=0),
        name="spread_receivers",
    )(positions, values, *args)
    spread = inject.reshape(STEPS, ext_x, ext_y, depth)

    corner = jax.ShapeDtypeStruct((2, Y_TILES, CORNER, PAD, depth), f32)
    corners = pl.pallas_call(
        corner_kernel,
        out_shape=(corner, corner),
        in_specs=[ANY] * 3,
        out_specs=(VMEM, VMEM),
        scratch_shapes=[pltpu.SemaphoreType.DMA((4,))],
        compiler_params=big,
        name="pack_corners",
    )(halos[2], halos[3], inject)
    halos += [lax.ppermute(corners[n], "gx", swaps_x[n]) for n in range(2)]

    def piece(strips, group):
        return jax.ShapeDtypeStruct((strips, len(group), strip_rows, width_y, depth), f32)

    first = tuple(range(early))
    groups = [tuple(range(i, min(i + 3, held))) for i in range(early, held, 3)]
    edge_rows = 2 * sum(HALF - v for v in VALID)
    edge = jax.ShapeDtypeStruct((edge_rows, width_y, depth), f32)
    step_ops = 30 * width_x * width_y * depth * STEPS
    tables = (owner, aperture)
    middle = (width_x - 2 * HALF) // strip_rows
    count = shots if early else 0
    inner = pl.pallas_call(
        functools.partial(inner_kernel, early, shots),
        out_shape=(piece(middle, first),) * count + (padded,) + (step,) * 3,
        in_specs=[SMEM] * 4 + [ANY] * 2 + [VMEM] * 2,
        out_specs=(VMEM,) * (count + 4),
        scratch_shapes=[pltpu.SemaphoreType.DMA((10,))],
        input_output_aliases={7: count},
        compiler_params=big,
        cost_estimate=pl.CostEstimate(flops=step_ops, bytes_accessed=12 * 2**20, transcendentals=0),
        name="inner_steps",
    )(*tables, src_pos, src_amp, *halos[2:4], spread, ext)
    inner_pieces, inner = inner[:count], inner[count:]
    outer = pl.pallas_call(
        functools.partial(outer_kernel, early, shots),
        out_shape=(piece(tiles - middle, first),) * count + (padded,) + (step,) * 3 + (edge, edge),
        in_specs=[SMEM] * 4 + [ANY] * 4 + [VMEM] * 5,
        out_specs=(VMEM,) * (count + 6),
        scratch_shapes=[pltpu.SemaphoreType.DMA((30,)), pltpu.SemaphoreType.DMA((12,))],
        input_output_aliases={9 + n: count + n for n in range(4)},
        compiler_params=big,
        cost_estimate=pl.CostEstimate(flops=step_ops, bytes_accessed=12 * 2**20, transcendentals=0),
        name="outer_steps",
    )(*tables, src_pos, src_amp, *halos[:2], *halos[4:], spread, *inner)
    outer_pieces, outer, edges = outer[:count], outer[count + 1 : count + 4], outer[count + 4 :]
    edges = [lax.ppermute(edges[n], "gx", swaps_x[n]) for n in range(2)]
    field = jax.ShapeDtypeStruct(src_cur.shape, f32)

    def others(part, *operands):
        strips = middle if part == 0 else tiles - middle
        shapes = [piece(strips, g).shape for g in groups for _ in range(shots)]
        extra = (field, field) if part == 0 else (step,) * 3
        result = pl.pallas_call(
            functools.partial(rest_kernel, part, groups, shots),
            out_shape=(jax.ShapeDtypeStruct(shapes[0], f32),)
            + tuple(pltpu.HBM(shape, f32) for shape in shapes[1:])
            + extra,
            in_specs=[SMEM] * 2 + ([VMEM] * 3 if part == 0 else [ANY] * 2 + [VMEM] * 3 + [ANY]),
            out_specs=(VMEM,) + (ANY,) * (len(shapes) - 1) + ((ANY,) * 2 if part == 0 else (VMEM,) * 3),
            scratch_shapes=[pltpu.VMEM(shape, f32) for shape in shapes[1:]]
            + [pltpu.SemaphoreType.DMA((12,)), pltpu.SemaphoreType.DMA((2 + held * shots,))],
            input_output_aliases={4 + n: len(shapes) + n for n in range(3 * part)},
            compiler_params=big,
            cost_estimate=pl.CostEstimate(
                flops=5 * OFFS * width_x * width_y * depth, bytes_accessed=12 * 2**20, transcendentals=0),
            name=("far_strips", "near_strips")[part],
        )(*tables, *operands)
        return result[: len(shapes)], result[len(shapes) :]

    def swapped(cells):
        return [
            lax.ppermute(one, "shot", [(s, (s + r + 1) % shots) for s in range(shots)])
            for r, one in enumerate(cells)
        ]

    def summed(part, kept, coming, group, old, cost):
        cells = list(kept[part]) + list(coming[part])
        return pl.pallas_call(
            functools.partial(sum_kernel, part, shots),
            out_shape=piece(tiles, group),
            in_specs=[SMEM] + [VMEM] * shots + [ANY] * part,
            out_specs=ANY,
            scratch_shapes=[
                pltpu.VMEM(cells[0].shape, f32), pltpu.SemaphoreType.DMA((cells[0].shape[0],))],
            input_output_aliases={1 + shots: 0} if part else {},
            compiler_params=small,
            cost_estimate=pl.CostEstimate(flops=cost[part], bytes_accessed=2**20, transcendentals=0),
            name=("sum_far", "sum_near")[part],
        )(owner, *cells, *old)

    totals = []
    coming = []
    if early:
        both = (inner_pieces, outer_pieces)
        coming = [swapped(cells[1:]) for cells in both]
        kept = [cells[:1] for cells in both]
        half = summed(0, kept, coming, first, [], SUM_COSTS[0])
        totals.append(summed(1, kept, coming, first, [half], SUM_COSTS[0]))
    far, (src_next, rcv_next) = others(0, *outer)
    near, _ = others(1, *edges, *outer, totals[0] if early else edges[0])
    half = None
    for g, group in enumerate(groups):
        both = [cells[g * shots : (g + 1) * shots] for cells in (far, near)]
        going = [cells[1:] for cells in both]
        if half is not None:
            (going, coming, half) = lax.optimization_barrier((going, coming, half))
            totals.append(summed(1, kept, coming, groups[g - 1], [half], SUM_COSTS[min(g, 2)]))
        elif coming:
            (going[0], coming) = lax.optimization_barrier((going[0], coming))
        coming = [swapped(cells) for cells in going]
        kept = [cells[:1] for cells in both]
        half = summed(0, kept, coming, group, [], SUM_COSTS[min(g + 1, 2)])
    totals.append(summed(1, kept, coming, groups[-1], [half], SUM_COSTS[min(len(groups), 2)]))
    gathers = jnp.zeros((1, held, tiles, strip_rows, width_y, depth), f32)
    chunks = ([first] if early else []) + groups
    for n, (group, total) in enumerate(zip(chunks, totals)):
        arrived = lax.all_to_all(total, ("gx", "gy"), split_axis=0, concat_axis=0, tiled=True)
        if n < len(chunks) - 1:
            for slot, i in enumerate(group):
                where = jnp.where(2 * shot < shots, held - 1 - i, i)
                gathers = lax.dynamic_update_slice(gathers, arrived[None, None, :, slot], (0, where, 0, 0, 0, 0))
            continue
        gathers = pl.pallas_call(
            functools.partial(place_kernel, group, held),
            out_shape=jax.ShapeDtypeStruct(gathers.shape, f32),
            in_specs=[ANY, VMEM],
            out_specs=ANY,
            scratch_shapes=[pltpu.SemaphoreType.DMA((len(group),))],
            input_output_aliases={0: 0},
            compiler_params=small,
            name="place_strips",
        )(gathers, arrived)
    return src_next, rcv_next, gathers


def solution(mesh):
    return jax.shard_map(
        body,
        mesh=mesh,
        in_specs=(
            P("gx", "gy", None),
            P("shot", "gx", "gy", None),
            P("shot", "gx", "gy", None),
            P("shot", "gx", "gy", None),
            P("shot", "gx", "gy", None),
            P("shot"),
            P("shot", None),
            P("shot", None),
            P("shot", None, None),
            P("shot", None),
            P(),
        ),
        out_specs=(
            P("shot", "gx", "gy", None),
            P("shot", "gx", "gy", None),
            P(("gx", "gy"), "shot", None, None, None, None),
        ),
        check_vma=False,
    )
```
